128 devices in a mesh: dp: 2 (over core), graph: 64 (over z, x, y).
Axes of the slice: x: 4, y: 4, z: 4, core: 2. Of those that a mesh axis runs over, the one named last changes fastest.
Arguments:
- grid_latent: bfloat16 [2, 131072, 512], P('dp', 'graph'), may hold values from -6 to 6
- mesh_init: bfloat16 [2, 16384, 512], P('dp', 'graph'), may hold values from -6 to 6
- cotangent: bfloat16 [2, 131072, 512], P('dp', 'graph'), may hold values from -6 to 6
- enc_senders: int32 [12, 16384], P(None, 'graph'), may hold values from 0 to 131071, as said below
- enc_counts: int32 [16384], P('graph'), may hold values from 3 to 12, as said below
- dec_senders: int32 [3, 131072], P(None, 'graph'), may hold values from 0 to 16383, as said below
- recv_weight: bfloat16 [512, 512], replicated, may hold values from -0.25 to 0.25
- send_weight: bfloat16 [512, 512], replicated, may hold values from -0.25 to 0.25
- update_weight: bfloat16 [512, 512], replicated, may hold values from -0.25 to 0.25
- norm_gain: bfloat16 [512], replicated, may hold values from 0.099609375 to 1.8984375
- mesh_send_weight: bfloat16 [512, 512], replicated, may hold values from -0.25 to 0.25
- grid_recv_weight: bfloat16 [512, 512], replicated, may hold values from -0.25 to 0.25
- output_weight: bfloat16 [512, 512], replicated, may hold values from -0.25 to 0.25
Outputs:
- grid_grad: bfloat16 [2, 131072, 512], P('dp', 'graph')
- mesh_grad: bfloat16 [2, 16384, 512], P('dp', 'graph')
- recv_grad: float32 [512, 512], replicated
- send_grad: float32 [512, 512], replicated
- update_grad: float32 [512, 512], replicated
- gain_grad: float32 [512], replicated
- msend_grad: float32 [512, 512], replicated
- grecv_grad: float32 [512, 512], replicated
- out_grad: float32 [512, 512], replicated
The draws below stay inside these ranges and needn't reach their ends.
Inputs may be any that keep to these rules, and one draw needn't show every extreme that they name: For mesh node m of patch p = m // 256 and position q = m % 256, every enc_senders[k, m] lies in [p * 2048 + q * 8 - 256, p * 2048 + (q + 1) * 8 + 256); slots k >= enc_counts[m] are padding. `enc_counts`: mesh nodes of the first and last 64 // 4 patches have 3 * 3 to 12 edges, the others 12 // 4 to 6. For grid node g of band b = g // 2048 and position q = g % 2048, every dec_senders[j, g] lies in [b * 256 + q * 256 // 2048 - 64, b * 256 + q * 256 // 2048 + 64].
All inputs are finite; a program needn't handle non-finite values.
Results may differ from the reference program's by a relative error of at most 0.02.
Values may be sent and summed in bfloat16 or wider, within the bound.
A program may use at most 192 MiB of HBM per device.

```python
import math
import jax
import jax.numpy as jnp
from jax import lax

D = 512
GR = 2048
MR = 256
KE = 12
GRIM = 256
MRIM = 64
SAMPLES = 2
BANDS = 64
GRID = 131072
MESH = 16384


def draw_enc_senders(key, part):
    key = jax.random.fold_in(key, 11)
    node_ids = jnp.arange(MESH, dtype=jnp.int32)
    patch_id = node_ids // MR
    position = node_ids % MR
    centre = patch_id * GR + position * GR // MR
    offset = jax.random.randint(key, (KE, MESH), -GRIM, GRIM + GR // MR, dtype=jnp.int32)
    first_slot = jnp.arange(KE, dtype=jnp.int32)[:, None] == 0
    offset = jnp.where(first_slot & (position == 0)[None, :], -GRIM, offset)
    offset = jnp.where(first_slot & (position == MR - 1)[None, :], GRIM + GR // MR - 1, offset)
    return jnp.clip(centre[None, :] + offset, 0, GRID - 1).astype(jnp.int32)


def draw_enc_counts(key, part):
    key = jax.random.fold_in(key, 23)
    node_ids = jnp.arange(MESH, dtype=jnp.int32)
    patch_id = node_ids // MR
    polar_patch = (patch_id < BANDS // 4) | (patch_id >= BANDS - BANDS // 4)
    lowest = jnp.where(polar_patch, KE - KE // 4, KE // 4)
    extra_edges = jax.random.randint(key, (MESH,), 0, KE // 4 + 1, dtype=jnp.int32)
    extra_edges = jnp.where(node_ids % MR == 0, KE // 4, extra_edges)
    return (lowest + extra_edges).astype(jnp.int32)


def draw_dec_senders(key, part):
    key = jax.random.fold_in(key, 17)
    cell_ids = jnp.arange(GRID, dtype=jnp.int32)
    band_id = cell_ids // GR
    position = cell_ids % GR
    centre = band_id * MR + position * MR // GR
    offset = jax.random.randint(key, (3, GRID), -MRIM, MRIM + 1, dtype=jnp.int32)
    first_slot = jnp.arange(3, dtype=jnp.int32)[:, None] == 0
    offset = jnp.where(first_slot & (position == 0)[None, :], -MRIM, offset)
    offset = jnp.where(first_slot & (position == GR - 1)[None, :], MRIM, offset)
    return jnp.clip(centre[None, :] + offset, 0, MESH - 1).astype(jnp.int32)


def steps_of(key, extent, split, least, top_value):
    level, own = 1.0, jax.random.fold_in(key, 6)
    for dim, parts in split:
        heights = jnp.exp(jax.random.uniform(jax.random.fold_in(own, dim), (parts,), jnp.float32, least / len(split), top_value / len(split)))
        level = level * jnp.repeat(heights, extent[dim] // parts).reshape([-1 if axis == dim else 1 for axis in range(len(extent))])
    return level


def gaussian(own_key, shape, scale, most, split=(), held_as=jnp.bfloat16):
    level = steps_of(own_key, shape, split, -0.22, 0.18) if split else 1.0
    entries = jax.random.normal(own_key, shape, jnp.float32) * scale * level
    return jnp.minimum(jnp.maximum(entries, -most), most).astype(held_as)


def setup_inputs(seed: int = 0) -> dict:
    streams_of = jax.random.split(jax.random.key(seed), 14)
    return {
        "grid_latent": gaussian(streams_of[0], (SAMPLES, GRID, D), 1.0, 6.0, ((0, 2), (1, 64))),
        "mesh_init": gaussian(streams_of[1], (SAMPLES, MESH, D), 1.0, 6.0, ((0, 2), (1, 64))),
        "cotangent": gaussian(streams_of[2], (SAMPLES, GRID, D), 1.0, 6.0, ((0, 2), (1, 64))),
        "enc_senders": draw_enc_senders(jax.random.fold_in(streams_of[13], 71), 0),
        "enc_counts": draw_enc_counts(jax.random.fold_in(streams_of[13], 71), 0),
        "dec_senders": draw_dec_senders(jax.random.fold_in(streams_of[13], 71), 0),
        "recv_weight": gaussian(streams_of[6], (D, D), D ** -0.5, 0.25),
        "send_weight": gaussian(streams_of[7], (D, D), D ** -0.5, 0.25),
        "update_weight": gaussian(streams_of[8], (D, D), D ** -0.5, 0.25),
        "norm_gain": jnp.clip(1.0 + 0.18 * jax.random.normal(streams_of[9], (D,), jnp.float32), 0.099609375, 1.8984375).astype(jnp.bfloat16),
        "mesh_send_weight": gaussian(streams_of[10], (D, D), D ** -0.5, 0.25),
        "grid_recv_weight": gaussian(streams_of[11], (D, D), D ** -0.5, 0.25),
        "output_weight": gaussian(streams_of[12], (D, D), D ** -0.5, 0.25),
    }


def activation(pre_value):
    gate_sig = jax.nn.sigmoid(pre_value)
    return (pre_value * gate_sig, gate_sig * (1.0 + pre_value * (1.0 - gate_sig)))

def dot_rows(left, right):
    return lax.dot_general(left, right, (((0,), (0,)), ((), ())), preferred_element_type=jnp.float32)

def dot_cols(left, right):
    return lax.dot_general(left, right, (((1,), (1,)), ((), ())), preferred_element_type=jnp.float32)

def reference(grid_latent, mesh_init, cotangent, enc_senders, enc_counts, dec_senders, recv_weight, send_weight, update_weight, norm_gain, mesh_send_weight, grid_recv_weight, output_weight):
    live_mask = (jnp.arange(KE, dtype=jnp.int32)[:, None] < enc_counts[None, :]).astype(jnp.float32)
    grads = [jnp.zeros((D, D), jnp.float32) for count_index in range(7)]
    grads[3] = jnp.zeros((D,), jnp.float32)
    grid_grads = []
    mesh_grads = []
    for sample in range(SAMPLES):
        grid_in = grid_latent[sample]
        mesh_in = mesh_init[sample]
        grid_cot = cotangent[sample]
        send_proj = jnp.dot(grid_in, send_weight, preferred_element_type=jnp.float32).astype(jnp.bfloat16)
        recv_proj = jnp.dot(mesh_in, recv_weight, preferred_element_type=jnp.float32).astype(jnp.bfloat16)
        aggregate = jnp.zeros((MESH, D), jnp.float32)
        for slot_index in range(KE):
            enc_pre = send_proj[enc_senders[slot_index]].astype(jnp.float32) + recv_proj.astype(jnp.float32)
            value, slope = activation(enc_pre)
            aggregate = aggregate + value * live_mask[slot_index][:, None]
        aggregate = aggregate.astype(jnp.bfloat16)
        update = jnp.dot(aggregate, update_weight, preferred_element_type=jnp.float32)
        inv_rms = lax.rsqrt(lax.optimization_barrier(jnp.mean(update * update, axis=-1, keepdims=True)) + 1e-06)
        normed = update * inv_rms
        mesh_latent = (mesh_in.astype(jnp.float32) + norm_gain.astype(jnp.float32) * normed).astype(jnp.bfloat16)
        mesh_proj = jnp.dot(mesh_latent, mesh_send_weight, preferred_element_type=jnp.float32).astype(jnp.bfloat16)
        grid_proj = jnp.dot(grid_in, grid_recv_weight, preferred_element_type=jnp.float32)
        dec_sum = jnp.zeros((GRID, D), jnp.float32)
        for sender_slot in range(3):
            dec_pre = mesh_proj[dec_senders[sender_slot]].astype(jnp.float32) + grid_proj
            value, slope = activation(dec_pre)
            dec_sum = dec_sum + value
        dec_sum = dec_sum.astype(jnp.bfloat16)
        out_term = dot_rows(dec_sum, grid_cot)
        sum_cot = dot_cols(grid_cot, output_weight)
        recv_cot = jnp.zeros((GRID, D), jnp.float32)
        mesh_cot = jnp.zeros((MESH, D), jnp.float32)
        for sender_slot in range(3):
            dec_pre = mesh_proj[dec_senders[sender_slot]].astype(jnp.float32) + grid_proj
            value, slope = activation(dec_pre)
            dec_cot = lax.optimization_barrier((sum_cot * slope).astype(jnp.bfloat16)).astype(jnp.float32)
            recv_cot = recv_cot + dec_cot
            mesh_cot = mesh_cot.at[dec_senders[sender_slot]].add(dec_cot)
        recv_cot = recv_cot.astype(jnp.bfloat16)
        mesh_cot = mesh_cot.astype(jnp.bfloat16)
        grecv_term = dot_rows(grid_in, recv_cot)
        msend_term = dot_rows(mesh_latent, mesh_cot)
        latent_cot = dot_cols(mesh_cot, mesh_send_weight)
        gain_term = lax.optimization_barrier(jnp.sum(latent_cot * normed, axis=0))
        normed_cot = latent_cot * norm_gain.astype(jnp.float32)
        update_cot = ((normed_cot - normed * lax.optimization_barrier(jnp.mean(normed_cot * normed, axis=-1, keepdims=True))) * inv_rms).astype(jnp.bfloat16)
        update_term = dot_rows(aggregate, update_cot)
        agg_cot = dot_cols(update_cot, update_weight)
        recv_sum = jnp.zeros((MESH, D), jnp.float32)
        send_cot = jnp.zeros((GRID, D), jnp.float32)
        for slot_index in range(KE):
            enc_pre = send_proj[enc_senders[slot_index]].astype(jnp.float32) + recv_proj.astype(jnp.float32)
            value, slope = activation(enc_pre)
            enc_cot = lax.optimization_barrier((agg_cot * slope * live_mask[slot_index][:, None]).astype(jnp.bfloat16)).astype(jnp.float32)
            recv_sum = recv_sum + enc_cot
            send_cot = send_cot.at[enc_senders[slot_index]].add(enc_cot)
        recv_sum = recv_sum.astype(jnp.bfloat16)
        send_cot = send_cot.astype(jnp.bfloat16)
        recv_term = dot_rows(mesh_in, recv_sum)
        send_term = dot_rows(grid_in, send_cot)
        mesh_grads.append((latent_cot + dot_cols(recv_sum, recv_weight)).astype(jnp.bfloat16))
        grid_total = grid_cot.astype(jnp.float32) + dot_cols(recv_cot, grid_recv_weight) + dot_cols(send_cot, send_weight)
        grid_grads.append(grid_total.astype(jnp.bfloat16))
        terms = [recv_term, send_term, update_term, gain_term, msend_term, grecv_term, out_term]
        grads = [grads[term_index] + terms[term_index] for term_index in range(7)]
    factor = 1.0 / math.sqrt(SAMPLES * GRID)
    return (jnp.stack(grid_grads), jnp.stack(mesh_grads), grads[0] * factor, grads[1] * factor, grads[2] * factor, grads[3] * factor, grads[4] * factor, grads[5] * factor, grads[6] * factor)
```

```python
import math

import jax
import jax.numpy as jnp
from jax import lax
from jax.experimental import pallas as pl
from jax.experimental.pallas import tpu as pltpu
from jax.sharding import PartitionSpec as P

KE = 12
GRIM = 256
MRIM = 64


def with_halo(block, sides, width):
    for axis, dim in sides:
        count = lax.axis_size(axis)
        forward = [(i, i + 1) for i in range(count - 1)]
        backward = [(target, source) for source, target in forward]
        low = lax.ppermute(
            lax.slice_in_dim(block, block.shape[dim] - width, None, axis=dim), axis, forward
        )
        high = lax.ppermute(lax.slice_in_dim(block, 0, width, axis=dim), axis, backward)
        block = jnp.concatenate([low, block, high], axis=dim)
    return block


def activation(pre_value):
    gate_sig = jax.nn.sigmoid(pre_value)
    return (pre_value * gate_sig, gate_sig * (1.0 + pre_value * (1.0 - gate_sig)))


def dot_rows(left, right):
    return lax.dot_general(
        left, right, (((0,), (0,)), ((), ())), preferred_element_type=jnp.float32
    )


def dot_cols(left, right):
    return lax.dot_general(
        left, right, (((1,), (1,)), ((), ())), preferred_element_type=jnp.float32
    )


def selector_block(index, number, block, numer, denom, width):
    window_start = number * block * numer // denom
    picked = lax.dynamic_slice_in_dim(index, number * block, block, 1) - window_start
    selector = (picked[..., None] == jnp.arange(width, dtype=jnp.int32)).astype(jnp.bfloat16)
    return (window_start, selector)


def window_take(extended, index, block, numer, denom, width):
    slots, columns = index.shape
    blocks = columns // block

    def one_block(number):
        window_start, selector = selector_block(index, number, block, numer, denom, width)
        window = lax.dynamic_slice_in_dim(extended, window_start, width, 0)
        return jnp.einsum(
            "smw,wd->smd", selector, window, preferred_element_type=jnp.float32
        ).astype(jnp.bfloat16)

    taken = lax.map(one_block, jnp.arange(blocks, dtype=jnp.int32))
    return jnp.transpose(taken, (1, 0, 2, 3)).reshape(slots, columns, extended.shape[1])


def window_add(total_rows, index, values, block, numer, denom, width):
    columns = index.shape[1]
    blocks = columns // block

    def one_block(totals, number):
        window_start, selector = selector_block(index, number, block, numer, denom, width)
        part_values = lax.dynamic_slice_in_dim(values, number * block, block, 1)
        added = jnp.einsum("smw,smd->wd", selector, part_values, preferred_element_type=jnp.float32)
        current = lax.dynamic_slice_in_dim(totals, window_start, width, 0)
        return (lax.dynamic_update_slice_in_dim(totals, current + added, window_start, 0), 0)

    start_totals = jnp.zeros((total_rows, values.shape[2]), jnp.float32)
    totals, unused = lax.scan(one_block, start_totals, jnp.arange(blocks, dtype=jnp.int32))
    return totals


def neighbour_rows(values, depth):
    return with_halo(values, (("graph", 0),), depth)


def return_rims(extended, depth):
    rims = jnp.concatenate([extended[:depth], extended[-depth:]], 0)
    arrived = with_halo(rims, (("graph", 0),), depth)
    owned = extended[depth:-depth]
    owned = owned.at[:depth].add(arrived[:depth])
    return owned.at[-depth:].add(arrived[-depth:])


def slot_forward(gathered, receiver, live_mask):
    enc_pre = gathered.astype(jnp.float32) + receiver.astype(jnp.float32)[None]
    value, slope = activation(enc_pre)
    return (jnp.sum(value * live_mask[..., None], axis=0), slope * live_mask[..., None])


STRIDES = (16, 4, 1)
ORDERS = ((0, 1, 2), (1, 2, 0), (2, 0, 1))


def remote(src, dst, sems, target):
    return pltpu.make_async_remote_copy(
        src_ref=src,
        dst_ref=dst,
        send_sem=sems.at[0],
        recv_sem=sems.at[1],
        device_id=target,
        device_id_type=pl.DeviceIdType.MESH,
    )


def sum_kernel(
    grads, gain, out, gain_out, pair_in, part, r1, s2, r2, s3, r3, gain_in, gain_held,
    pair_sem, rs_sem, ag_sem, last_sem, gain_sem
):
    core = lax.axis_index("dp")
    place = lax.axis_index("graph")
    coords = [lax.rem(place // stride, 4) for stride in STRIDES]

    def peer(axis, offset):
        moved = lax.rem(coords[axis] + offset, 4)
        return moved, {"graph": place + (moved - coords[axis]) * STRIDES[axis]}

    barrier = pltpu.get_barrier_semaphore()
    pl.semaphore_signal(
        barrier, inc=1, device_id={"dp": 1 - core}, device_id_type=pl.DeviceIdType.MESH
    )
    for axis in range(3):
        for offset in (1, 2, 3):
            pl.semaphore_signal(
                barrier,
                inc=1,
                device_id=peer(axis, offset)[1],
                device_id_type=pl.DeviceIdType.MESH,
            )
    pl.semaphore_wait(barrier, 10)

    pair = []
    for p in range(3):
        copy = remote(
            grads.at[3 * (1 - core) + p], pair_in.at[p], pair_sem.at[p], {"dp": 1 - core}
        )
        copy.start()
        pair.append(copy)
    gain_copy = remote(gain, gain_in.at[9], gain_sem.at[9], {"dp": 1 - core})
    gain_copy.start()
    sent = [gain_copy]
    stages = []
    for p in range(3):
        pair[p].wait_recv()
        part[p] = (
            grads[3 * core + p].astype(jnp.float32) + pair_in[p].astype(jnp.float32)
        ).astype(jnp.bfloat16)
        axis = ORDERS[p][0]
        for offset in (1, 2, 3):
            moved, target = peer(axis, offset)
            copy = remote(
                part.at[p, pl.ds(pl.multiple_of(moved * 128, 128), 128)],
                r1.at[p, offset - 1],
                rs_sem.at[p, offset - 1],
                target,
            )
            copy.start()
            stages.append(copy)
    sent += pair
    gain_copy.wait_recv()
    gain_held[0] = gain[...] + gain_in[9]
    for step in range(3):
        copies = []
        for offset in (1, 2, 3):
            slot = 3 * step + offset - 1
            copy = remote(
                gain_held.at[step], gain_in.at[slot], gain_sem.at[slot], peer(step, offset)[1]
            )
            copy.start()
            copies.append(copy)
        if step == 0:
            second = []
            for p in range(3):
                for copy in stages[3 * p : 3 * p + 3]:
                    copy.wait_recv()
                mine = coords[ORDERS[p][0]]
                total = part[p, pl.ds(pl.multiple_of(mine * 128, 128), 128)].astype(jnp.float32)
                for slot in range(3):
                    total = total + r1[p, slot].astype(jnp.float32)
                s2[p] = total.astype(jnp.bfloat16)
                for offset in (1, 2, 3):
                    moved, target = peer(ORDERS[p][1], offset)
                    copy = remote(
                        s2.at[p, pl.ds(pl.multiple_of(moved * 32, 32), 32)],
                        r2.at[p, offset - 1],
                        rs_sem.at[3 + p, offset - 1],
                        target,
                    )
                    copy.start()
                    second.append(copy)
            sent += stages
        if step == 1:
            third = []
            for p in range(3):
                for copy in second[3 * p : 3 * p + 3]:
                    copy.wait_recv()
                mine = coords[ORDERS[p][1]]
                total = s2[p, pl.ds(pl.multiple_of(mine * 32, 32), 32)].astype(jnp.float32)
                for slot in range(3):
                    total = total + r2[p, slot].astype(jnp.float32)
                total = total.astype(jnp.bfloat16)
                for quarter in range(4):
                    s3[p, quarter] = total[
                        16 * (quarter // 2) : 16 * (quarter // 2) + 16,
                        256 * (quarter % 2) : 256 * (quarter % 2) + 256,
                    ]
                for offset in (1, 2, 3):
                    moved, target = peer(ORDERS[p][2], offset)
                    copy = remote(
                        s3.at[p, moved], r3.at[p, offset - 1], rs_sem.at[6 + p, offset - 1], target
                    )
                    copy.start()
                    third.append(copy)
            sent += second
        for copy in copies:
            copy.wait_recv()
        sent += copies
        total = gain_held[step]
        for slot in range(3):
            total = total + gain_in[3 * step + slot]
        if step < 2:
            gain_held[step + 1] = total
        else:
            gain_out[...] = total
    sent += third

    def spread(p, level, slot, piece):
        copies = []
        for offset in (1, 2, 3):
            copy = remote(
                piece, piece, ag_sem.at[3 * level + p, offset - 1], peer(ORDERS[p][level], offset)[1]
            )
            copy.start()
            copies.append(copy)
        return copies

    rows3, rows2, rows1 = [], [], []
    wave = []
    for p in range(3):
        for copy in third[3 * p : 3 * p + 3]:
            copy.wait_recv()
        first, middle, last = [coords[axis] for axis in ORDERS[p]]
        total = s3[p, last].astype(jnp.float32)
        for slot in range(3):
            total = total + r3[p, slot].astype(jnp.float32)
        row1 = pl.multiple_of(first * 128, 128)
        row2 = pl.multiple_of(first * 128 + middle * 32, 32)
        row3 = pl.multiple_of(first * 128 + middle * 32 + (last // 2) * 16, 16)
        column = pl.multiple_of(lax.rem(last, 2) * 256, 256)
        whole = out.at[3 * core + p]
        rows1.append(whole.at[pl.ds(row1, 128)])
        rows2.append(whole.at[pl.ds(row2, 32)])
        piece = whole.at[pl.ds(row3, 16), pl.ds(column, 256)]
        piece[...] = total.astype(jnp.bfloat16)
        wave.append(spread(p, 2, 0, piece))
    for level, pieces in ((1, rows2), (0, rows1)):
        following = []
        for p in range(3):
            for copy in wave[p]:
                copy.wait_recv()
            following.append(spread(p, level, 0, pieces[p]))
            sent += wave[p]
        wave = following
    last = []
    for p in range(3):
        for copy in wave[p]:
            copy.wait_recv()
        copy = remote(
            out.at[3 * core + p], out.at[3 * core + p], last_sem.at[p], {"dp": 1 - core}
        )
        copy.start()
        last.append(copy)
        sent += wave[p]
    for copy in last:
        copy.wait_recv()
    sent += last
    for copy in sent:
        copy.wait_send()


def sum_everywhere(grads, gain):
    half = jnp.bfloat16
    return pl.pallas_call(
        sum_kernel,
        out_shape=(
            jax.ShapeDtypeStruct((6, 512, 512), half),
            jax.ShapeDtypeStruct((8, 128), jnp.float32),
        ),
        in_specs=[pl.BlockSpec(memory_space=pltpu.VMEM)] * 2,
        out_specs=[pl.BlockSpec(memory_space=pltpu.VMEM)] * 2,
        scratch_shapes=[
            pltpu.VMEM((3, 512, 512), half),
            pltpu.VMEM((3, 512, 512), half),
            pltpu.VMEM((3, 3, 128, 512), half),
            pltpu.VMEM((3, 128, 512), half),
            pltpu.VMEM((3, 3, 32, 512), half),
            pltpu.VMEM((3, 4, 16, 256), half),
            pltpu.VMEM((3, 3, 16, 256), half),
            pltpu.VMEM((10, 8, 128), jnp.float32),
            pltpu.VMEM((3, 8, 128), jnp.float32),
            pltpu.SemaphoreType.DMA((3, 2)),
            pltpu.SemaphoreType.DMA((9, 3, 2)),
            pltpu.SemaphoreType.DMA((9, 3, 2)),
            pltpu.SemaphoreType.DMA((3, 2)),
            pltpu.SemaphoreType.DMA((10, 2)),
        ],
        compiler_params=pltpu.CompilerParams(
            collective_id=0, has_side_effects=True, vmem_limit_bytes=48 * 1024 * 1024
        ),
    )(grads, gain)


def shards(
    grid_latent,
    mesh_init,
    cotangent,
    enc_senders,
    enc_counts,
    dec_senders,
    recv_weight,
    send_weight,
    update_weight,
    norm_gain,
    mesh_send_weight,
    grid_recv_weight,
    output_weight,
):
    band_index = lax.axis_index("graph")
    grid_in = grid_latent[0]
    mesh_in = mesh_init[0]
    grid_cot = cotangent[0]
    grid_rows = grid_in.shape[0]
    mesh_rows = mesh_in.shape[0]
    ratio_rows = grid_rows // mesh_rows
    enc_block = min(mesh_rows, 128)
    enc_width = enc_block * ratio_rows + 2 * GRIM
    dec_block = min(grid_rows, 512)
    dec_width = dec_block // ratio_rows + 2 * MRIM
    send_proj = jnp.dot(grid_in, send_weight, preferred_element_type=jnp.float32).astype(
        jnp.bfloat16
    )
    send_ext = neighbour_rows(send_proj, GRIM)
    recv_proj = jnp.dot(mesh_in, recv_weight, preferred_element_type=jnp.float32).astype(
        jnp.bfloat16
    )
    local_index = enc_senders - (band_index * grid_rows - GRIM)
    live_mask = (jnp.arange(KE, dtype=jnp.int32)[:, None] < enc_counts[None, :]).astype(jnp.float32)
    agg_total, deriv_all = slot_forward(
        window_take(send_ext, local_index, enc_block, ratio_rows, 1, enc_width),
        recv_proj,
        live_mask,
    )
    aggregate = agg_total.astype(jnp.bfloat16)
    update = jnp.dot(aggregate, update_weight, preferred_element_type=jnp.float32)
    inv_rms = lax.rsqrt(jnp.mean(update * update, axis=-1, keepdims=True) + 1e-06)
    normed = update * inv_rms
    mesh_latent = (mesh_in.astype(jnp.float32) + norm_gain.astype(jnp.float32) * normed).astype(
        jnp.bfloat16
    )
    mesh_proj = jnp.dot(mesh_latent, mesh_send_weight, preferred_element_type=jnp.float32).astype(
        jnp.bfloat16
    )
    mesh_ext = neighbour_rows(mesh_proj, MRIM)
    dec_index = dec_senders - (band_index * mesh_rows - MRIM)
    grid_proj = jnp.dot(grid_in, grid_recv_weight, preferred_element_type=jnp.float32)
    dec_rows = window_take(mesh_ext, dec_index, dec_block, 1, ratio_rows, dec_width)
    dec_pre = dec_rows.astype(jnp.float32) + grid_proj[None]
    dec_value, dec_slope = activation(dec_pre)
    dec_sum = jnp.sum(dec_value, axis=0).astype(jnp.bfloat16)
    out_term = dot_rows(dec_sum, grid_cot)
    sum_cot = dot_cols(grid_cot, output_weight)
    dec_narrow = lax.optimization_barrier((sum_cot[None] * dec_slope).astype(jnp.bfloat16))
    recv_cot = jnp.sum(dec_narrow.astype(jnp.float32), axis=0).astype(jnp.bfloat16)
    mesh_cot_ext = window_add(
        mesh_rows + 2 * MRIM, dec_index, dec_narrow, dec_block, 1, ratio_rows, dec_width
    )
    mesh_cot = return_rims(mesh_cot_ext, MRIM).astype(jnp.bfloat16)
    grecv_term = dot_rows(grid_in, recv_cot)
    msend_term = dot_rows(mesh_latent, mesh_cot)
    latent_cot = dot_cols(mesh_cot, mesh_send_weight)
    gain_term = jnp.sum(latent_cot * normed, axis=0)
    normed_cot = latent_cot * norm_gain.astype(jnp.float32)
    update_cot = (
        (normed_cot - normed * jnp.mean(normed_cot * normed, axis=-1, keepdims=True)) * inv_rms
    ).astype(jnp.bfloat16)
    update_term = dot_rows(aggregate, update_cot)
    agg_cot = dot_cols(update_cot, update_weight)
    enc_cot = (agg_cot[None] * deriv_all).astype(jnp.bfloat16)
    enc_cot = lax.optimization_barrier(enc_cot)
    recv_sum = jnp.sum(enc_cot.astype(jnp.float32), axis=0).astype(jnp.bfloat16)
    send_cot_ext = window_add(
        grid_rows + 2 * GRIM, local_index, enc_cot, enc_block, ratio_rows, 1, enc_width
    )
    send_cot = return_rims(send_cot_ext, GRIM).astype(jnp.bfloat16)
    recv_term = dot_rows(mesh_in, recv_sum)
    send_term = dot_rows(grid_in, send_cot)
    mesh_grad = (latent_cot + dot_cols(recv_sum, recv_weight)).astype(jnp.bfloat16)[None]
    grid_total = (
        grid_cot.astype(jnp.float32)
        + dot_cols(recv_cot, grid_recv_weight)
        + dot_cols(send_cot, send_weight)
    )
    grid_grad = grid_total.astype(jnp.bfloat16)[None]
    terms = (recv_term, send_term, update_term, msend_term, grecv_term, out_term)
    stacked = jnp.stack([term.astype(jnp.bfloat16) for term in terms])
    gain_rows = jnp.concatenate([gain_term.reshape(4, 128), jnp.zeros((4, 128), jnp.float32)])
    totals, gain_total = sum_everywhere(stacked, gain_rows)
    totals = totals.astype(jnp.float32)
    factor = 1.0 / math.sqrt(grid_rows * lax.axis_size("graph") * lax.axis_size("dp"))
    return (
        grid_grad,
        mesh_grad,
        totals[0] * factor,
        totals[1] * factor,
        totals[2] * factor,
        gain_total[:4].reshape(512) * factor,
        totals[3] * factor,
        totals[4] * factor,
        totals[5] * factor,
    )


def solution(mesh):
    return jax.shard_map(
        shards,
        mesh=mesh,
        in_specs=(
            P("dp", "graph", None),
            P("dp", "graph", None),
            P("dp", "graph", None),
            P(None, "graph"),
            P("graph"),
            P(None, "graph"),
            P(),
            P(),
            P(),
            P(),
            P(),
            P(),
            P(),
        ),
        out_specs=(
            P("dp", "graph", None),
            P("dp", "graph", None),
            P(),
            P(),
            P(),
            P(),
            P(),
            P(),
            P(),
        ),
        check_vma=False,
    )
```

```python
import math

import jax
import jax.numpy as jnp
from jax import lax
from jax.experimental import pallas as pl
from jax.experimental.pallas import tpu as pltpu
from jax.sharding import PartitionSpec as P

KE = 12
GRIM = 256
MRIM = 64


STRIDES = (16, 4, 1)
ORDERS = ((0, 1, 2), (1, 2, 0), (2, 0, 1))


def remote(src, dst, sems, target):
    return pltpu.make_async_remote_copy(
        src_ref=src,
        dst_ref=dst,
        send_sem=sems.at[0],
        recv_sem=sems.at[1],
        device_id=target,
        device_id_type=pl.DeviceIdType.MESH,
    )


def sum_kernel(
    grads, gain, out, gain_out, pair_in, part, r1, s2, r2, s3, r3, gain_in, gain_held,
    pair_sem, rs_sem, ag_sem, last_sem, gain_sem
):
    core = lax.axis_index("dp")
    place = lax.axis_index("graph")
    coords = [lax.rem(place // stride, 4) for stride in STRIDES]

    def peer(axis, offset):
        moved = lax.rem(coords[axis] + offset, 4)
        return moved, {"graph": place + (moved - coords[axis]) * STRIDES[axis]}

    barrier = pltpu.get_barrier_semaphore()
    pl.semaphore_signal(
        barrier, inc=1, device_id={"dp": 1 - core}, device_id_type=pl.DeviceIdType.MESH
    )
    for axis in range(3):
        for offset in (1, 2, 3):
            pl.semaphore_signal(
                barrier,
                inc=1,
                device_id=peer(axis, offset)[1],
                device_id_type=pl.DeviceIdType.MESH,
            )
    pl.semaphore_wait(barrier, 10)

    pair = []
    for p in range(3):
        copy = remote(
            grads.at[3 * (1 - core) + p], pair_in.at[p], pair_sem.at[p], {"dp": 1 - core}
        )
        copy.start()
        pair.append(copy)
    gain_copy = remote(gain, gain_in.at[9], gain_sem.at[9], {"dp": 1 - core})
    gain_copy.start()
    sent = [gain_copy]
    stages = []
    for p in range(3):
        pair[p].wait_recv()
        part[p] = (
            grads[3 * core + p].astype(jnp.float32) + pair_in[p].astype(jnp.float32)
        ).astype(jnp.bfloat16)
        axis = ORDERS[p][0]
        for offset in (1, 2, 3):
            moved, target = peer(axis, offset)
            copy = remote(
                part.at[p, pl.ds(pl.multiple_of(moved * 128, 128), 128)],
                r1.at[p, offset - 1],
                rs_sem.at[p, offset - 1],
                target,
            )
            copy.start()
            stages.append(copy)
    sent += pair
    gain_copy.wait_recv()
    gain_held[0] = gain[...] + gain_in[9]
    for step in range(3):
        copies = []
        for offset in (1, 2, 3):
            slot = 3 * step + offset - 1
            copy = remote(
                gain_held.at[step], gain_in.at[slot], gain_sem.at[slot], peer(step, offset)[1]
            )
            copy.start()
            copies.append(copy)
        if step == 0:
            second = []
            for p in range(3):
                for copy in stages[3 * p : 3 * p + 3]:
                    copy.wait_recv()
                mine = coords[ORDERS[p][0]]
                total = part[p, pl.ds(pl.multiple_of(mine * 128, 128), 128)].astype(jnp.float32)
                for slot in range(3):
                    total = total + r1[p, slot].astype(jnp.float32)
                s2[p] = total.astype(jnp.bfloat16)
                for offset in (1, 2, 3):
                    moved, target = peer(ORDERS[p][1], offset)
                    copy = remote(
                        s2.at[p, pl.ds(pl.multiple_of(moved * 32, 32), 32)],
                        r2.at[p, offset - 1],
                        rs_sem.at[3 + p, offset - 1],
                        target,
                    )
                    copy.start()
                    second.append(copy)
            sent += stages
        if step == 1:
            third = []
            for p in range(3):
                for copy in second[3 * p : 3 * p + 3]:
                    copy.wait_recv()
                mine = coords[ORDERS[p][1]]
                total = s2[p, pl.ds(pl.multiple_of(mine * 32, 32), 32)].astype(jnp.float32)
                for slot in range(3):
                    total = total + r2[p, slot].astype(jnp.float32)
                total = total.astype(jnp.bfloat16)
                for quarter in range(4):
                    s3[p, quarter] = total[
                        16 * (quarter // 2) : 16 * (quarter // 2) + 16,
                        256 * (quarter % 2) : 256 * (quarter % 2) + 256,
                    ]
                for offset in (1, 2, 3):
                    moved, target = peer(ORDERS[p][2], offset)
                    copy = remote(
                        s3.at[p, moved], r3.at[p, offset - 1], rs_sem.at[6 + p, offset - 1], target
                    )
                    copy.start()
                    third.append(copy)
            sent += second
        for copy in copies:
            copy.wait_recv()
        sent += copies
        total = gain_held[step]
        for slot in range(3):
            total = total + gain_in[3 * step + slot]
        if step < 2:
            gain_held[step + 1] = total
        else:
            gain_out[...] = total
    sent += third

    def spread(p, level, slot, piece):
        copies = []
        for offset in (1, 2, 3):
            copy = remote(
                piece, piece, ag_sem.at[3 * level + p, offset - 1], peer(ORDERS[p][level], offset)[1]
            )
            copy.start()
            copies.append(copy)
        return copies

    rows3, rows2, rows1 = [], [], []
    wave = []
    for p in range(3):
        for copy in third[3 * p : 3 * p + 3]:
            copy.wait_recv()
        first, middle, last = [coords[axis] for axis in ORDERS[p]]
        total = s3[p, last].astype(jnp.float32)
        for slot in range(3):
            total = total + r3[p, slot].astype(jnp.float32)
        row1 = pl.multiple_of(first * 128, 128)
        row2 = pl.multiple_of(first * 128 + middle * 32, 32)
        row3 = pl.multiple_of(first * 128 + middle * 32 + (last // 2) * 16, 16)
        column = pl.multiple_of(lax.rem(last, 2) * 256, 256)
        whole = out.at[3 * core + p]
        rows1.append(whole.at[pl.ds(row1, 128)])
        rows2.append(whole.at[pl.ds(row2, 32)])
        piece = whole.at[pl.ds(row3, 16), pl.ds(column, 256)]
        piece[...] = total.astype(jnp.bfloat16)
        wave.append(spread(p, 2, 0, piece))
    for level, pieces in ((1, rows2), (0, rows1)):
        following = []
        for p in range(3):
            for copy in wave[p]:
                copy.wait_recv()
            following.append(spread(p, level, 0, pieces[p]))
            sent += wave[p]
        wave = following
    last = []
    for p in range(3):
        for copy in wave[p]:
            copy.wait_recv()
        copy = remote(
            out.at[3 * core + p], out.at[3 * core + p], last_sem.at[p], {"dp": 1 - core}
        )
        copy.start()
        last.append(copy)
        sent += wave[p]
    for copy in last:
        copy.wait_recv()
    sent += last
    for copy in sent:
        copy.wait_send()


def sum_everywhere(grads, gain):
    half = jnp.bfloat16
    return pl.pallas_call(
        sum_kernel,
        out_shape=(
            jax.ShapeDtypeStruct((6, 512, 512), half),
            jax.ShapeDtypeStruct((8, 128), jnp.float32),
        ),
        in_specs=[pl.BlockSpec(memory_space=pltpu.VMEM)] * 2,
        out_specs=[pl.BlockSpec(memory_space=pltpu.VMEM)] * 2,
        scratch_shapes=[
            pltpu.VMEM((3, 512, 512), half),
            pltpu.VMEM((3, 512, 512), half),
            pltpu.VMEM((3, 3, 128, 512), half),
            pltpu.VMEM((3, 128, 512), half),
            pltpu.VMEM((3, 3, 32, 512), half),
            pltpu.VMEM((3, 4, 16, 256), half),
            pltpu.VMEM((3, 3, 16, 256), half),
            pltpu.VMEM((10, 8, 128), jnp.float32),
            pltpu.VMEM((3, 8, 128), jnp.float32),
            pltpu.SemaphoreType.DMA((3, 2)),
            pltpu.SemaphoreType.DMA((9, 3, 2)),
            pltpu.SemaphoreType.DMA((9, 3, 2)),
            pltpu.SemaphoreType.DMA((3, 2)),
            pltpu.SemaphoreType.DMA((10, 2)),
        ],
        compiler_params=pltpu.CompilerParams(
            collective_id=0, has_side_effects=True, vmem_limit_bytes=48 * 1024 * 1024
        ),
    )(grads, gain)


HALF = jnp.bfloat16
FULL = jnp.float32
NODES = 32
DEPTH = KE * NODES
REACH = NODES * 8 + 2 * GRIM
CELLS = 512
SPAN = CELLS // 8 + 2 * MRIM


def dot(left, right, dims=((1,), (0,))):
    return lax.dot_general(left, right, (dims, ((), ())), preferred_element_type=FULL)


def loop(count, body, start=0):
    lax.fori_loop(start, count, lambda step, carry: (body(step), carry)[1], 0)


def rows_at(index, size):
    return pl.ds(pl.multiple_of(index * size, size), size)


def half_silu(half_pre):
    bend = jnp.tanh(half_pre)
    lifted = 1.0 + bend
    value = half_pre * lifted
    return value, lifted + value * (1.0 - bend)


def local_kernel(
    grid, mesh, cot, enc_col, enc_row, counts, dec_col, dec_row,
    w_recv, w_send, w_update, gain, w_msend, w_grecv, w_out,
    grid_grad, mesh_grad, terms, gain_rows,
    send_ext, gp, sc, rp, taken, slope, agg, normed, inv, mlat, mesh_ext,
    dcot, dsum, rcot, mc_ext, mesh_rim, lat, mcot, ucot, acot, ecot, rsum,
    scot, rim_out, rim_in, edge, acc, sems,
):
    place = lax.axis_index("graph")
    left = {"graph": lax.rem(place + 63, 64)}
    right = {"graph": lax.rem(place + 1, 64)}
    barrier = pltpu.get_barrier_semaphore()
    for target in (left, right):
        pl.semaphore_signal(
            barrier, inc=1, device_id=target, device_id_type=pl.DeviceIdType.MESH
        )
    pl.semaphore_wait(barrier, 2)
    sent = []

    def exchange(index, low, low_target, high, high_target):
        pair = [
            remote(low, low_target, sems.at[index], left),
            remote(high, high_target, sems.at[index + 1], right),
        ]
        for copy in pair:
            copy.start()
        sent.extend(pair)
        return pair

    def project(start, size):
        send_ext[pl.ds(start + GRIM, size)] = (
            dot(grid[pl.ds(start, size)], w_send[...]) * 0.5
        ).astype(HALF)

    project(0, GRIM)
    project(2048 - GRIM, GRIM)
    grid_halo = exchange(
        0,
        send_ext.at[pl.ds(GRIM, GRIM)],
        send_ext.at[pl.ds(2048 + GRIM, GRIM)],
        send_ext.at[pl.ds(2048, GRIM)],
        send_ext.at[pl.ds(0, GRIM)],
    )
    loop(3, lambda step: project(pl.multiple_of(GRIM + step * 512, 256), 512))
    rp[...] = dot(mesh[...], w_recv[...]).astype(HALF).astype(FULL) * 0.5

    def dense(step):
        rows = rows_at(step, 512)
        gp[rows] = dot(grid[rows], w_grecv[...]) * 0.5
        sc[rows] = dot(cot[rows], w_out[...], ((1,), (1,))) * 0.5

    loop(4, dense)

    def encode(number):
        columns = lax.broadcasted_iota(jnp.int32, (NODES, REACH), 1) + number * (NODES * 8)
        nodes = rows_at(number, NODES)
        picks = enc_col[nodes]
        selector = jnp.concatenate(
            [
                jnp.where(picks[:, k : k + 1] == columns, 1.0, 0.0).astype(HALF)
                for k in range(KE)
            ]
        )
        taken[pl.ds(0, DEPTH)] = dot(
            selector, send_ext[pl.ds(pl.multiple_of(number * (NODES * 8), 256), REACH)]
        )
        for part in range(NODES // 16):
            rows = pl.ds(pl.multiple_of(number * NODES + part * 16, 16), 16)
            number_live = counts[rows]
            receiver = rp[rows]
            total = jnp.zeros((16, 512), FULL)
            for k in range(KE):
                at = k * NODES + part * 16
                value, bend = half_silu(taken[at : at + 16] + receiver)
                mask = jnp.where(number_live > k, 1.0, 0.0)
                total = total + value * mask
                slope[number, at : at + 16] = (bend * mask).astype(HALF)
            agg[rows] = total.astype(HALF)

    loop(7, encode, 1)
    for copy in grid_halo:
        copy.wait_recv()
    loop(2, lambda step: encode(step * 7))

    acot[...] = dot(agg[...], w_update[...])

    def normalise(step):
        rows = rows_at(step, 16)
        update = acot[rows]
        scale = lax.rsqrt(jnp.mean(update * update, axis=-1, keepdims=True) + 1e-06)
        inv[rows] = jnp.broadcast_to(scale, (16, 128))
        flat = update * scale
        normed[rows] = flat
        mlat[rows] = (mesh[rows].astype(FULL) + gain[...].astype(FULL) * flat).astype(HALF)

    loop(16, normalise)
    mesh_ext[pl.ds(MRIM, 256)] = (dot(mlat[...], w_msend[...]) * 0.5).astype(HALF)
    mesh_halo = exchange(
        2,
        mesh_ext.at[pl.ds(MRIM, MRIM)],
        mesh_ext.at[pl.ds(256 + MRIM, MRIM)],
        mesh_ext.at[pl.ds(256, MRIM)],
        mesh_ext.at[pl.ds(0, MRIM)],
    )
    mc_ext[...] = jnp.zeros_like(mc_ext)

    def decode(number):
        base = pl.multiple_of(number * (CELLS // 8), 64)
        cells = rows_at(number, CELLS)
        window = mesh_ext[pl.ds(base, SPAN)]
        columns = lax.broadcasted_iota(jnp.int32, (CELLS, SPAN), 1) + base
        picks = dec_col[cells]
        for j in range(3):
            selector = jnp.where(picks[:, j : j + 1] == columns, 1.0, 0.0).astype(HALF)
            taken[pl.ds(j * CELLS, CELLS)] = dot(selector, window)

        def cell_rows(step):
            inner = rows_at(step, 16)
            rows = pl.ds(pl.multiple_of(number * CELLS + step * 16, 16), 16)
            own = gp[rows]
            cotangent = sc[rows]
            total = jnp.zeros((16, 512), FULL)
            back = jnp.zeros((16, 512), FULL)
            for j in range(3):
                value, bend = half_silu(
                    taken[pl.ds(pl.multiple_of(j * CELLS + step * 16, 16), 16)] + own
                )
                total = total + value
                part = cotangent * bend
                back = back + part
                dcot[j, inner] = part.astype(HALF)
            dsum[rows] = total.astype(HALF)
            rcot[rows] = back.astype(HALF)

        lax.fori_loop(0, CELLS // 16, lambda i, c: (cell_rows(i), c)[1], 0, unroll=4)
        lines = lax.broadcasted_iota(jnp.int32, (SPAN, CELLS), 0) + base
        added = mc_ext[pl.ds(base, SPAN)]
        for j in range(3):
            selector = jnp.where(dec_row[j, number] == lines, 1.0, 0.0).astype(HALF)
            added = added + dot(selector, dcot[j])
        mc_ext[pl.ds(base, SPAN)] = added

    loop(3, decode, 1)
    for copy in mesh_halo:
        copy.wait_recv()
    loop(2, lambda step: decode(step * 3))
    mesh_back = exchange(
        4,
        mc_ext.at[pl.ds(0, MRIM)],
        mesh_rim.at[1],
        mc_ext.at[pl.ds(256 + MRIM, MRIM)],
        mesh_rim.at[0],
    )

    def contract(slot, lefts, rights, count, size):
        acc[...] = jnp.zeros_like(acc)

        def piece(step):
            rows = rows_at(step, size)
            acc[...] += dot(lefts[rows], rights[rows], ((0,), (0,)))

        loop(count, piece)
        terms[slot] = acc[...].astype(HALF)

    contract(5, dsum, cot, 4, 512)
    contract(4, grid, rcot, 4, 512)

    def first_part(step):
        rows = rows_at(step, 512)
        gp[rows] = cot[rows].astype(FULL) + dot(rcot[rows], w_grecv[...], ((1,), (1,)))

    loop(4, first_part)
    for copy in mesh_back:
        copy.wait_recv()
    mcot[pl.ds(0, MRIM)] = (mc_ext[pl.ds(MRIM, MRIM)] + mesh_rim[0]).astype(HALF)
    mcot[pl.ds(MRIM, 128)] = mc_ext[pl.ds(2 * MRIM, 128)].astype(HALF)
    mcot[pl.ds(192, MRIM)] = (mc_ext[pl.ds(256, MRIM)] + mesh_rim[1]).astype(HALF)
    lat[...] = dot(mcot[...], w_msend[...], ((1,), (1,)))
    gain_rows[...] = jnp.zeros_like(gain_rows)

    def unnormalise(step, total):
        rows = rows_at(step, 16)
        flat = normed[rows]
        product = lat[rows] * flat
        scaled = lat[rows] * gain[...].astype(FULL)
        mean = jnp.mean(scaled * flat, axis=-1, keepdims=True)
        ucot[rows] = ((scaled - flat * mean) * inv[rows][:, :1]).astype(HALF)
        return total + product[:8] + product[8:]

    gain_total = lax.fori_loop(0, 16, unnormalise, jnp.zeros((8, 512), FULL))
    gain_sum = jnp.sum(gain_total, axis=0, keepdims=True)
    for part in range(4):
        gain_rows[part : part + 1, :] = gain_sum[:, 128 * part : 128 * part + 128]
    acot[...] = dot(ucot[...], w_update[...], ((1,), (1,))) * 0.5

    def encode_back(number):
        for part in range(NODES // 16):
            rows = pl.ds(pl.multiple_of(number * NODES + part * 16, 16), 16)
            cotangent = acot[rows]
            total = jnp.zeros((16, 512), FULL)
            for k in range(KE):
                at = k * NODES + part * 16
                piece = cotangent * slope[number, at : at + 16].astype(FULL)
                total = total + piece
                ecot[number, at : at + 16] = piece.astype(HALF)
            rsum[rows] = total.astype(HALF)

    def scatter(tile, numbers):
        total = None
        for number in numbers:
            lines = lax.broadcasted_iota(jnp.int32, (256, DEPTH), 0) + tile * 256
            selector = jnp.where(enc_row[number] == lines, 1.0, 0.0).astype(HALF)
            piece = dot(selector, ecot[number])
            total = piece if total is None else total + piece
        return total

    loop(2, lambda step: encode_back(step * 7))
    rim_out[0] = scatter(0, (0,)).astype(HALF)
    rim_out[1] = scatter(9, (7,)).astype(HALF)
    grid_back = exchange(6, rim_out.at[0], rim_in.at[1], rim_out.at[1], rim_in.at[0])
    loop(7, encode_back, 1)
    edge[0] = scatter(1, (0, 1))
    edge[1] = scatter(8, (6, 7))

    def inner_tile(tile):
        scot[pl.ds(pl.multiple_of((tile - 1) * 256, 256), 256)] = scatter(
            tile, (tile - 2, tile - 1, tile)
        ).astype(HALF)

    loop(8, inner_tile, 2)
    contract(0, mesh, rsum, 1, 256)
    contract(2, agg, ucot, 1, 256)
    contract(3, mlat, mcot, 1, 256)
    mesh_grad[...] = (lat[...] + dot(rsum[...], w_recv[...], ((1,), (1,)))).astype(HALF)
    for copy in grid_back:
        copy.wait_recv()
    scot[pl.ds(0, GRIM)] = (edge[0] + rim_in[0].astype(FULL)).astype(HALF)
    scot[pl.ds(2048 - GRIM, GRIM)] = (edge[1] + rim_in[1].astype(FULL)).astype(HALF)
    contract(1, grid, scot, 4, 512)

    def last_part(step):
        rows = rows_at(step, 512)
        grid_grad[rows] = (gp[rows] + dot(scot[rows], w_send[...], ((1,), (1,)))).astype(HALF)

    loop(4, last_part)
    for copy in sent:
        copy.wait_send()


def local_work(*operands):
    vmem = pltpu.VMEM
    return pl.pallas_call(
        local_kernel,
        out_shape=(
            jax.ShapeDtypeStruct((2048, 512), HALF),
            jax.ShapeDtypeStruct((256, 512), HALF),
            jax.ShapeDtypeStruct((6, 512, 512), HALF),
            jax.ShapeDtypeStruct((8, 128), FULL),
        ),
        in_specs=[pl.BlockSpec(memory_space=vmem)] * len(operands),
        out_specs=[pl.BlockSpec(memory_space=vmem)] * 4,
        scratch_shapes=[
            vmem((2048 + 2 * GRIM, 512), HALF),
            vmem((2048, 512), FULL),
            vmem((2048, 512), FULL),
            vmem((256, 512), FULL),
            vmem((3 * CELLS, 512), FULL),
            vmem((8, DEPTH, 512), HALF),
            vmem((256, 512), HALF),
            vmem((256, 512), FULL),
            vmem((256, 128), FULL),
            vmem((256, 512), HALF),
            vmem((256 + 2 * MRIM, 512), HALF),
            vmem((3, CELLS, 512), HALF),
            vmem((2048, 512), HALF),
            vmem((2048, 512), HALF),
            vmem((256 + 2 * MRIM, 512), FULL),
            vmem((2, MRIM, 512), FULL),
            vmem((256, 512), FULL),
            vmem((256, 512), HALF),
            vmem((256, 512), HALF),
            vmem((256, 512), FULL),
            vmem((8, DEPTH, 512), HALF),
            vmem((256, 512), HALF),
            vmem((2048, 512), HALF),
            vmem((2, GRIM, 512), HALF),
            vmem((2, GRIM, 512), HALF),
            vmem((2, GRIM, 512), FULL),
            vmem((512, 512), FULL),
            pltpu.SemaphoreType.DMA((8, 2)),
        ],
        compiler_params=pltpu.CompilerParams(
            collective_id=1, has_side_effects=True, vmem_limit_bytes=60 * 1024 * 1024
        ),
    )(*operands)


def shards(
    grid_latent,
    mesh_init,
    cotangent,
    enc_senders,
    enc_counts,
    dec_senders,
    recv_weight,
    send_weight,
    update_weight,
    norm_gain,
    mesh_send_weight,
    grid_recv_weight,
    output_weight,
):
    band_index = lax.axis_index("graph")
    enc_index = enc_senders - (band_index * 2048 - GRIM)
    dec_index = dec_senders - (band_index * 256 - MRIM)
    enc_row = enc_index.reshape(KE, 8, NODES).transpose(1, 0, 2).reshape(8, 1, DEPTH)
    dec_row = dec_index.reshape(3, 4, 1, CELLS)
    grid_grad, mesh_grad, stacked, gain_rows = local_work(
        grid_latent[0],
        mesh_init[0],
        cotangent[0],
        enc_index.T,
        enc_row,
        enc_counts.reshape(256, 1),
        dec_index.T,
        dec_row,
        recv_weight,
        send_weight,
        update_weight,
        norm_gain.reshape(1, 512),
        mesh_send_weight,
        grid_recv_weight,
        output_weight,
    )
    totals, gain_total = sum_everywhere(stacked, gain_rows)
    totals = totals.astype(FULL)
    factor = 1.0 / math.sqrt(2048 * lax.axis_size("graph") * lax.axis_size("dp"))
    return (
        grid_grad[None],
        mesh_grad[None],
        totals[0] * factor,
        totals[1] * factor,
        totals[2] * factor,
        gain_total[:4].reshape(512) * factor,
        totals[3] * factor,
        totals[4] * factor,
        totals[5] * factor,
    )


def solution(mesh):
    return jax.shard_map(
        shards,
        mesh=mesh,
        in_specs=(
            P("dp", "graph", None),
            P("dp", "graph", None),
            P("dp", "graph", None),
            P(None, "graph"),
            P("graph"),
            P(None, "graph"),
            P(),
            P(),
            P(),
            P(),
            P(),
            P(),
            P(),
        ),
        out_specs=(
            P("dp", "graph", None),
            P("dp", "graph", None),
            P(),
            P(),
            P(),
            P(),
            P(),
            P(),
            P(),
        ),
        check_vma=False,
    )
```

```python
import math

import jax
import jax.numpy as jnp
from jax import lax
from jax.experimental import pallas as pl
from jax.experimental.pallas import tpu as pltpu
from jax.sharding import PartitionSpec as P

KE = 12
GRIM = 256
MRIM = 64


STRIDES = (16, 4, 1)
ORDERS = ((0, 1, 2), (1, 2, 0), (2, 0, 1))


def remote(src, dst, sems, target):
    return pltpu.make_async_remote_copy(
        src_ref=src,
        dst_ref=dst,
        send_sem=sems.at[0],
        recv_sem=sems.at[1],
        device_id=target,
        device_id_type=pl.DeviceIdType.MESH,
    )


HALF = jnp.bfloat16
FULL = jnp.float32
NODES = 32
DEPTH = KE * NODES
REACH = NODES * 8 + 2 * GRIM
CELLS = 512
SPAN = CELLS // 8 + 2 * MRIM
PARTS = ((0, 256), (256, 128), (384, 128))


def dot(left, right, dims=((1,), (0,))):
    return lax.dot_general(left, right, (dims, ((), ())), preferred_element_type=FULL)


def loop(count, body, start=0):
    lax.fori_loop(start, count, lambda step, carry: (body(step), carry)[1], 0)


def rows_at(index, size):
    return pl.ds(pl.multiple_of(index * size, size), size)


def half_silu(half_pre):
    bend = jnp.tanh(half_pre)
    lifted = 1.0 + bend
    value = half_pre * lifted
    return value, lifted + value * (1.0 - bend)


def whole_kernel(
    grid_any, mesh_any, cot_any, enc, counts, dec,
    w_recv_any, w_send_any, w_update_any, gain, w_msend_any, w_grecv_any, w_out_any,
    grid_grad, mesh_grad, totals, gain_total,
    grid_ext, mesh, cot, w_recv, w_send, w_update, w_msend, w_grecv, w_out,
    stage, enc_col, enc_row, dec_stage, dec_col,
    send_ext, gp, sc, rp, taken, slope, agg, normed, inv, mlat, mesh_ext,
    dcot, dsum, rcot, mc_ext, mesh_rim, lat, mcot, ucot, acot, rsum,
    scot, rim_in, acc, mgrad,
    terms, pair_in, paired, r1, s2, r2, r3, summed, gain_in, gain_held,
    load_sem, store_sem, sems, pair_sem, rs_sem, ag_sem, last_sem, gain_sem,
):
    core = lax.axis_index("dp")
    place = lax.axis_index("graph")
    twin = {"dp": 1 - core}
    left = {"graph": lax.rem(place + 63, 64)}
    right = {"graph": lax.rem(place + 1, 64)}
    coords = [lax.rem(place // stride, 4) for stride in STRIDES]

    def peer(axis, offset):
        moved = lax.rem(coords[axis] + offset, 4)
        return moved, {"graph": place + (moved - coords[axis]) * STRIDES[axis]}

    loads = {}
    for number, (name, source, target) in enumerate((
        ("w_send", w_send_any, w_send),
        ("grid", grid_any, grid_ext.at[pl.ds(GRIM, 2048)]),
        ("mesh", mesh_any, mesh),
        ("w_recv", w_recv_any, w_recv),
        ("w_grecv", w_grecv_any, w_grecv),
        ("cot", cot_any, cot),
        ("w_out", w_out_any, w_out),
        ("w_update", w_update_any, w_update),
        ("w_msend", w_msend_any, w_msend),
    )):
        loads[name] = pltpu.make_async_copy(source, target, load_sem.at[number])
        loads[name].start()

    barrier = pltpu.get_barrier_semaphore()
    targets = [left, right, twin]
    targets += [peer(axis, offset)[1] for axis in range(3) for offset in (1, 2, 3)]
    for target in targets:
        pl.semaphore_signal(
            barrier, inc=1, device_id=target, device_id_type=pl.DeviceIdType.MESH
        )
    pl.semaphore_wait(barrier, 12)
    sent = []

    def exchange(index, low, low_target, high, high_target):
        pair = [
            remote(low, low_target, sems.at[index], left),
            remote(high, high_target, sems.at[index + 1], right),
        ]
        for copy in pair:
            copy.start()
        sent.extend(pair)
        return pair

    grid_halo = exchange(
        0,
        grid_any.at[pl.ds(0, GRIM)],
        grid_ext.at[pl.ds(2048 + GRIM, GRIM)],
        grid_any.at[pl.ds(2048 - GRIM, GRIM)],
        grid_ext.at[pl.ds(0, GRIM)],
    )

    stage[...] = jnp.zeros_like(stage)
    stage[0:KE] = enc[...] - (place * 2048 - GRIM)
    stage[KE : KE + 1] = counts[...].reshape(1, 256)
    enc_col[...] = jnp.transpose(stage[...])
    for number in range(8):
        for k in range(KE):
            enc_row[number, :, k * NODES : (k + 1) * NODES] = stage[
                k : k + 1, number * NODES : (number + 1) * NODES
            ]
    dec_stage[...] = jnp.zeros_like(dec_stage)
    dec_stage[0:3] = dec[...] - (place * 256 - MRIM)
    dec_col[...] = jnp.transpose(dec_stage[...])

    def project(start, size):
        rows = pl.ds(start, size)
        send_ext[rows] = (dot(grid_ext[rows], w_send[...]) * 0.5).astype(HALF)

    loads["w_send"].wait()
    loads["grid"].wait()
    loop(4, lambda step: project(pl.multiple_of(GRIM + step * 512, 256), 512))
    loads["mesh"].wait()
    loads["w_recv"].wait()
    rp[...] = dot(mesh[...], w_recv[...]).astype(HALF).astype(FULL) * 0.5
    loads["w_grecv"].wait()
    loads["cot"].wait()
    loads["w_out"].wait()

    def dense(step):
        rows = rows_at(step, 512)
        shifted = pl.ds(pl.multiple_of(GRIM + step * 512, 256), 512)
        gp[rows] = dot(grid_ext[shifted], w_grecv[...]) * 0.5
        sc[rows] = dot(cot[rows], w_out[...], ((1,), (1,))) * 0.5

    loop(4, dense)

    def encode(number):
        columns = lax.broadcasted_iota(jnp.int32, (NODES, REACH), 1) + number * (NODES * 8)
        picks = enc_col[rows_at(number, NODES)]
        selector = jnp.concatenate(
            [
                jnp.where(picks[:, k : k + 1] == columns, 1.0, 0.0).astype(HALF)
                for k in range(KE)
            ]
        )
        taken[pl.ds(0, DEPTH)] = dot(
            selector, send_ext[pl.ds(pl.multiple_of(number * (NODES * 8), 256), REACH)]
        )
        for part in range(NODES // 16):
            rows = pl.ds(pl.multiple_of(number * NODES + part * 16, 16), 16)
            number_live = enc_col[rows][:, KE : KE + 1]
            receiver = rp[rows]
            total = jnp.zeros((16, 512), FULL)
            for k in range(KE):
                at = k * NODES + part * 16
                value, bend = half_silu(taken[at : at + 16] + receiver)
                mask = jnp.where(number_live > k, 1.0, 0.0)
                total = total + value * mask
                slope[number, at : at + 16] = (bend * mask).astype(HALF)
            agg[rows] = total.astype(HALF)

    loop(7, encode, 1)
    for copy in grid_halo:
        copy.wait_recv()
    project(0, GRIM)
    project(2048 + GRIM, GRIM)
    loop(2, lambda step: encode(step * 7))

    loads["w_update"].wait()
    acot[...] = dot(agg[...], w_update[...])
    wide_gain = gain[...].astype(FULL).reshape(1, 512)

    def normalise(step):
        rows = rows_at(step, 16)
        update = acot[rows]
        scale = lax.rsqrt(jnp.mean(update * update, axis=-1, keepdims=True) + 1e-06)
        inv[rows] = jnp.broadcast_to(scale, (16, 128))
        flat = update * scale
        normed[rows] = flat
        mlat[rows] = (mesh[rows].astype(FULL) + wide_gain * flat).astype(HALF)

    loop(16, normalise)
    loads["w_msend"].wait()
    mesh_ext[pl.ds(MRIM, 256)] = (dot(mlat[...], w_msend[...]) * 0.5).astype(HALF)
    mesh_halo = exchange(
        2,
        mesh_ext.at[pl.ds(MRIM, MRIM)],
        mesh_ext.at[pl.ds(256 + MRIM, MRIM)],
        mesh_ext.at[pl.ds(256, MRIM)],
        mesh_ext.at[pl.ds(0, MRIM)],
    )
    mc_ext[...] = jnp.zeros_like(mc_ext)

    def decode(number):
        base = pl.multiple_of(number * (CELLS // 8), 64)
        cells = rows_at(number, CELLS)
        window = mesh_ext[pl.ds(base, SPAN)]
        columns = lax.broadcasted_iota(jnp.int32, (CELLS, SPAN), 1) + base
        picks = dec_col[cells]
        for j in range(3):
            selector = jnp.where(picks[:, j : j + 1] == columns, 1.0, 0.0).astype(HALF)
            taken[pl.ds(j * CELLS, CELLS)] = dot(selector, window)

        def cell_rows(step):
            inner = rows_at(step, 16)
            rows = pl.ds(pl.multiple_of(number * CELLS + step * 16, 16), 16)
            own = gp[rows]
            cotangent = sc[rows]
            total = jnp.zeros((16, 512), FULL)
            back = jnp.zeros((16, 512), FULL)
            for j in range(3):
                value, bend = half_silu(
                    taken[pl.ds(pl.multiple_of(j * CELLS + step * 16, 16), 16)] + own
                )
                total = total + value
                part = cotangent * bend
                back = back + part
                dcot[j, inner] = part.astype(HALF)
            dsum[rows] = total.astype(HALF)
            rcot[rows] = back.astype(HALF)

        lax.fori_loop(0, CELLS // 16, lambda i, c: (cell_rows(i), c)[1], 0, unroll=4)
        lines = lax.broadcasted_iota(jnp.int32, (SPAN, CELLS), 0) + base
        added = mc_ext[pl.ds(base, SPAN)]
        for j in range(3):
            line = dec_stage[j : j + 1, pl.ds(pl.multiple_of(number * CELLS, CELLS), CELLS)]
            selector = jnp.where(line == lines, 1.0, 0.0).astype(HALF)
            added = added + dot(selector, dcot[j])
        mc_ext[pl.ds(base, SPAN)] = added

    loop(3, decode, 1)
    for copy in mesh_halo:
        copy.wait_recv()
    loop(2, lambda step: decode(step * 3))
    mesh_back = exchange(
        4,
        mc_ext.at[pl.ds(0, MRIM)],
        mesh_rim.at[1],
        mc_ext.at[pl.ds(256 + MRIM, MRIM)],
        mesh_rim.at[0],
    )

    def contract(slot, lefts, rights, count, size, shift=0):
        acc[...] = jnp.zeros_like(acc)

        def piece(step):
            rows = rows_at(step, size)
            moved = pl.ds(pl.multiple_of(step * size + shift, 256), size)
            acc[...] += dot(lefts[moved], rights[rows], ((0,), (0,)))

        loop(count, piece)
        terms[slot] = acc[...].astype(HALF)

    def fan(source, target, semaphores, axis):
        copies = []
        for offset in (1, 2, 3):
            moved, device = peer(axis, offset)
            copy = remote(source(moved), target(offset), semaphores.at[offset - 1], device)
            copy.start()
            copies.append(copy)
        sent.extend(copies)
        return copies

    def everywhere(group):
        own = 2 * group + core
        copy = remote(
            terms.at[2 * group + 1 - core], pair_in.at[group], pair_sem.at[group], twin
        )
        copy.start()
        sent.append(copy)
        yield
        copy.wait_recv()
        paired[group] = (terms[own].astype(FULL) + pair_in[group].astype(FULL)).astype(HALF)
        orders = [ORDERS[(p + group) % 3] for p in range(3)]
        columns = [pl.ds(*PARTS[p]) for p in range(3)]
        waves = [
            fan(
                lambda moved: paired.at[group, rows_at(moved, 128), columns[p]],
                lambda offset: r1.at[group, offset - 1, :, columns[p]],
                rs_sem.at[3 * group + p],
                orders[p][0],
            )
            for p in range(3)
        ]
        yield
        for p in range(3):
            for copy in waves[p]:
                copy.wait_recv()
            total = paired[group, rows_at(coords[orders[p][0]], 128), columns[p]].astype(FULL)
            for slot in range(3):
                total = total + r1[group, slot, :, columns[p]].astype(FULL)
            s2[group, :, columns[p]] = total.astype(HALF)
            waves[p] = fan(
                lambda moved: s2.at[group, rows_at(moved, 32), columns[p]],
                lambda offset: r2.at[group, offset - 1, :, columns[p]],
                rs_sem.at[9 + 3 * group + p],
                orders[p][1],
            )
        yield
        for p in range(3):
            for copy in waves[p]:
                copy.wait_recv()
            total = s2[group, rows_at(coords[orders[p][1]], 32), columns[p]].astype(FULL)
            for slot in range(3):
                total = total + r2[group, slot, :, columns[p]].astype(FULL)
            mine = coords[orders[p][2]]
            r3[group, mine, :, columns[p]] = total.astype(HALF)
            waves[p] = fan(
                lambda moved: r3.at[group, mine, :, columns[p]],
                lambda offset: r3.at[group, mine, :, columns[p]],
                rs_sem.at[18 + 3 * group + p],
                orders[p][2],
            )
        yield
        for p in range(3):
            for copy in waves[p]:
                copy.wait_recv()
            total = r3[group, 0, :, columns[p]].astype(FULL)
            for slot in range(1, 4):
                total = total + r3[group, slot, :, columns[p]].astype(FULL)
            number = coords[orders[p][0]] * 4 + coords[orders[p][1]]
            rows = rows_at(number, 32)
            summed[own, rows, columns[p]] = total.astype(HALF)
            piece = summed.at[own, rows, columns[p]]
            waves[p] = fan(
                lambda moved: piece, lambda offset: piece, ag_sem.at[3 * group + p], orders[p][1]
            )
        yield
        for p in range(3):
            for copy in waves[p]:
                copy.wait_recv()
            piece = summed.at[own, rows_at(coords[orders[p][0]], 128), columns[p]]
            waves[p] = fan(
                lambda moved: piece,
                lambda offset: piece,
                ag_sem.at[9 + 3 * group + p],
                orders[p][0],
            )
        yield
        last = []
        for p in range(3):
            for copy in waves[p]:
                copy.wait_recv()
            piece = summed.at[own, :, columns[p]]
            copy = remote(piece, piece, last_sem.at[group, p], twin)
            copy.start()
            last.append(copy)
        sent.extend(last)
        yield
        for copy in last:
            copy.wait_recv()
        copy = pltpu.make_async_copy(
            summed.at[pl.ds(2 * group, 2)],
            totals.at[pl.ds(2 * group, 2)],
            store_sem.at[group],
        )
        copy.start()
        stores.append(copy)
        yield

    def gain_everywhere():
        copy = remote(gain_held.at[0, 0], gain_in, gain_sem.at[9], twin)
        copy.start()
        sent.append(copy)
        yield
        copy.wait_recv()
        total = gain_held[0, 0] + gain_in[...]
        for step in range(3):
            mine = coords[step]
            gain_held[step + 1, mine] = total
            copies = []
            for offset in (1, 2, 3):
                piece = gain_held.at[step + 1, mine]
                copy = remote(
                    piece, piece, gain_sem.at[3 * step + offset - 1], peer(step, offset)[1]
                )
                copy.start()
                copies.append(copy)
            sent.extend(copies)
            yield
            for copy in copies:
                copy.wait_recv()
            total = gain_held[step + 1, 0]
            for slot in range(1, 4):
                total = total + gain_held[step + 1, slot]
        gain_total[...] = total
        yield

    stores = []
    running = []

    def pump(*chosen):
        for chain in chosen:
            next(chain)

    contract(0, grid_ext, rcot, 4, 512, GRIM)
    contract(1, dsum, cot, 4, 512)
    first = everywhere(0)
    second = everywhere(1)
    third = everywhere(2)
    fourth = gain_everywhere()
    pump(first)

    for copy in mesh_back:
        copy.wait_recv()
    mcot[pl.ds(0, MRIM)] = (mc_ext[pl.ds(MRIM, MRIM)] + mesh_rim[0]).astype(HALF)
    mcot[pl.ds(MRIM, 128)] = mc_ext[pl.ds(2 * MRIM, 128)].astype(HALF)
    mcot[pl.ds(192, MRIM)] = (mc_ext[pl.ds(256, MRIM)] + mesh_rim[1]).astype(HALF)
    lat[...] = dot(mcot[...], w_msend[...], ((1,), (1,)))
    gain_held[0, 0] = jnp.zeros((8, 128), FULL)

    def unnormalise(step, total):
        rows = rows_at(step, 16)
        flat = normed[rows]
        product = lat[rows] * flat
        scaled = lat[rows] * wide_gain
        mean = jnp.mean(scaled * flat, axis=-1, keepdims=True)
        ucot[rows] = ((scaled - flat * mean) * inv[rows][:, :1]).astype(HALF)
        return total + product[:8] + product[8:]

    rowwise = lax.fori_loop(0, 16, unnormalise, jnp.zeros((8, 512), FULL))
    gain_sum = jnp.sum(rowwise, axis=0, keepdims=True)
    for part in range(4):
        gain_held[0, 0, part : part + 1, :] = gain_sum[:, 128 * part : 128 * part + 128]
    acot[...] = dot(ucot[...], w_update[...], ((1,), (1,))) * 0.5
    pump(first)
    contract(2, agg, ucot, 1, 256)
    contract(3, mlat, mcot, 1, 256)
    pump(second, fourth)

    def encode_back(number):
        for part in range(NODES // 16):
            rows = pl.ds(pl.multiple_of(number * NODES + part * 16, 16), 16)
            cotangent = acot[rows]
            total = jnp.zeros((16, 512), FULL)
            for k in range(KE):
                at = k * NODES + part * 16
                piece = cotangent * slope[number, at : at + 16].astype(FULL)
                total = total + piece
                slope[number, at : at + 16] = piece.astype(HALF)
            rsum[rows] = total.astype(HALF)

    def scatter(tile, numbers):
        total = None
        for number in numbers:
            lines = lax.broadcasted_iota(jnp.int32, (256, DEPTH), 0) + tile * 256
            selector = jnp.where(enc_row[number] == lines, 1.0, 0.0).astype(HALF)
            piece = dot(selector, slope[number])
            total = piece if total is None else total + piece
        scot[rows_at(tile, 256)] = total.astype(HALF)

    loop(2, lambda step: encode_back(step * 7))
    scatter(0, (0,))
    scatter(9, (7,))
    grid_back = exchange(
        6,
        scot.at[pl.ds(0, GRIM)],
        rim_in.at[1],
        scot.at[pl.ds(2048 + GRIM, GRIM)],
        rim_in.at[0],
    )
    pump(first, second, fourth)
    loop(7, encode_back, 1)
    pump(first)
    scatter(1, (0, 1))
    scatter(8, (6, 7))
    pump(second, fourth)
    loop(5, lambda tile: scatter(tile, (tile - 2, tile - 1, tile)), 2)
    pump(first, fourth)
    loop(8, lambda tile: scatter(tile, (tile - 2, tile - 1, tile)), 5)
    pump(first, second)
    contract(4, mesh, rsum, 1, 256)
    contract(5, grid_ext, scot, 5, 512)
    pump(third, first, second, fourth)
    mgrad[...] = (lat[...] + dot(rsum[...], w_recv[...], ((1,), (1,)))).astype(HALF)
    copy = pltpu.make_async_copy(mgrad, mesh_grad, store_sem.at[3])
    copy.start()
    stores.append(copy)
    pump(third)

    def first_part(step):
        rows = rows_at(step, 512)
        gp[rows] = cot[rows].astype(FULL) + dot(rcot[rows], w_grecv[...], ((1,), (1,)))

    loop(2, first_part)
    pump(first, second)
    loop(4, first_part, 2)
    pump(third)
    for copy in grid_back:
        copy.wait_recv()
    for rim, start in ((0, GRIM), (1, 2048)):
        rows = pl.ds(start, GRIM)
        scot[rows] = (scot[rows].astype(FULL) + rim_in[rim].astype(FULL)).astype(HALF)

    def last_part(step):
        rows = rows_at(step, 512)
        shifted = pl.ds(pl.multiple_of(GRIM + step * 512, 256), 512)
        dsum[rows] = (gp[rows] + dot(scot[shifted], w_send[...], ((1,), (1,)))).astype(HALF)

    loop(2, last_part)
    pump(third, second)
    loop(4, last_part, 2)
    copy = pltpu.make_async_copy(dsum, grid_grad, store_sem.at[4])
    copy.start()
    stores.append(copy)
    for chain in (third, second, first, fourth):
        for unused in chain:
            pass
    for copy in sent:
        copy.wait_send()
    for copy in stores:
        copy.wait()


def everything(*operands):
    vmem = pltpu.VMEM
    anywhere = pl.BlockSpec(memory_space=pl.ANY)
    near = pl.BlockSpec(memory_space=vmem)
    return pl.pallas_call(
        whole_kernel,
        out_shape=(
            jax.ShapeDtypeStruct((2048, 512), HALF),
            jax.ShapeDtypeStruct((256, 512), HALF),
            jax.ShapeDtypeStruct((6, 512, 512), HALF),
            jax.ShapeDtypeStruct((8, 128), FULL),
        ),
        in_specs=[anywhere] * 3 + [near] * 3 + [anywhere] * 3 + [near] + [anywhere] * 3,
        out_specs=[anywhere, anywhere, anywhere, near],
        scratch_shapes=[
            vmem((2048 + 2 * GRIM, 512), HALF),
            vmem((256, 512), HALF),
            vmem((2048, 512), HALF),
        ]
        + [vmem((512, 512), HALF)] * 6
        + [
            vmem((16, 256), jnp.int32),
            vmem((256, 16), jnp.int32),
            vmem((8, 1, DEPTH), jnp.int32),
            vmem((8, 2048), jnp.int32),
            vmem((2048, 8), jnp.int32),
            vmem((2048 + 2 * GRIM, 512), HALF),
            vmem((2048, 512), FULL),
            vmem((2048, 512), FULL),
            vmem((256, 512), FULL),
            vmem((3 * CELLS, 512), FULL),
            vmem((8, DEPTH, 512), HALF),
            vmem((256, 512), HALF),
            vmem((256, 512), FULL),
            vmem((256, 128), FULL),
            vmem((256, 512), HALF),
            vmem((256 + 2 * MRIM, 512), HALF),
            vmem((3, CELLS, 512), HALF),
            vmem((2048, 512), HALF),
            vmem((2048, 512), HALF),
            vmem((256 + 2 * MRIM, 512), FULL),
            vmem((2, MRIM, 512), FULL),
            vmem((256, 512), FULL),
            vmem((256, 512), HALF),
            vmem((256, 512), HALF),
            vmem((256, 512), FULL),
            vmem((256, 512), HALF),
            vmem((2048 + 2 * GRIM, 512), HALF),
            vmem((2, GRIM, 512), HALF),
            vmem((512, 512), FULL),
            vmem((256, 512), HALF),
            vmem((6, 512, 512), HALF),
            vmem((3, 512, 512), HALF),
            vmem((3, 512, 512), HALF),
            vmem((3, 3, 128, 512), HALF),
            vmem((3, 128, 512), HALF),
            vmem((3, 3, 32, 512), HALF),
            vmem((3, 4, 32, 512), HALF),
            vmem((6, 512, 512), HALF),
            vmem((8, 128), FULL),
            vmem((4, 4, 8, 128), FULL),
            pltpu.SemaphoreType.DMA((9,)),
            pltpu.SemaphoreType.DMA((5,)),
            pltpu.SemaphoreType.DMA((8, 2)),
            pltpu.SemaphoreType.DMA((3, 2)),
            pltpu.SemaphoreType.DMA((27, 3, 2)),
            pltpu.SemaphoreType.DMA((18, 3, 2)),
            pltpu.SemaphoreType.DMA((3, 3, 2)),
            pltpu.SemaphoreType.DMA((10, 2)),
        ],
        compiler_params=pltpu.CompilerParams(
            collective_id=0, has_side_effects=True, vmem_limit_bytes=62 * 1024 * 1024
        ),
    )(*operands)


def shards(
    grid_latent,
    mesh_init,
    cotangent,
    enc_senders,
    enc_counts,
    dec_senders,
    recv_weight,
    send_weight,
    update_weight,
    norm_gain,
    mesh_send_weight,
    grid_recv_weight,
    output_weight,
):
    grid_grad, mesh_grad, totals, gain_total = everything(
        grid_latent[0],
        mesh_init[0],
        cotangent[0],
        enc_senders,
        enc_counts,
        dec_senders,
        recv_weight,
        send_weight,
        update_weight,
        norm_gain,
        mesh_send_weight,
        grid_recv_weight,
        output_weight,
    )
    totals = totals.astype(FULL)
    factor = 1.0 / math.sqrt(2048 * lax.axis_size("graph") * lax.axis_size("dp"))
    return (
        grid_grad[None],
        mesh_grad[None],
        totals[4] * factor,
        totals[5] * factor,
        totals[2] * factor,
        gain_total[:4].reshape(512) * factor,
        totals[3] * factor,
        totals[0] * factor,
        totals[1] * factor,
    )


def solution(mesh):
    return jax.shard_map(
        shards,
        mesh=mesh,
        in_specs=(
            P("dp", "graph", None),
            P("dp", "graph", None),
            P("dp", "graph", None),
            P(None, "graph"),
            P("graph"),
            P(None, "graph"),
            P(),
            P(),
            P(),
            P(),
            P(),
            P(),
            P(),
        ),
        out_specs=(
            P("dp", "graph", None),
            P("dp", "graph", None),
            P(),
            P(),
            P(),
            P(),
            P(),
            P(),
            P(),
        ),
        check_vma=False,
    )
```

```python
import functools
import math

import jax
import jax.numpy as jnp
from jax import lax
from jax.experimental import pallas as pl
from jax.experimental.pallas import tpu as pltpu
from jax.sharding import PartitionSpec as P

KE = 12
GRIM = 256
MRIM = 64


STRIDES = (16, 4, 1)
ORDERS = ((0, 1, 2), (1, 2, 0), (2, 0, 1))


def remote(src, dst, sems, target):
    return pltpu.make_async_remote_copy(
        src_ref=src,
        dst_ref=dst,
        send_sem=sems.at[0],
        recv_sem=sems.at[1],
        device_id=target,
        device_id_type=pl.DeviceIdType.MESH,
    )


HALF = jnp.bfloat16
FULL = jnp.float32
NODES = 32
DEPTH = KE * NODES
REACH = NODES * 8 + 2 * GRIM
CELLS = 512
SPAN = CELLS // 8 + 2 * MRIM
PARTS = ((0, 128), (128, 128), (256, 128), (384, 128))


def dot(left, right, dims=((1,), (0,))):
    return lax.dot_general(left, right, (dims, ((), ())), preferred_element_type=FULL)


def loop(count, body, start=0):
    lax.fori_loop(start, count, lambda step, carry: (body(step), carry)[1], 0)


def rows_at(index, size):
    return pl.ds(pl.multiple_of(index * size, size), size)


def half_silu(half_pre):
    bend = jnp.tanh(half_pre)
    lifted = 1.0 + bend
    value = half_pre * lifted
    return value, lifted + value * (1.0 - bend)


def whole_kernel(
    grid_any, mesh_any, cot_any, enc, counts, dec,
    w_recv_any, w_send_any, w_update_any, gain, w_msend_any, w_grecv_any, w_out_any,
    grid_grad, mesh_grad, totals, gain_total,
    grid_ext, mesh, cot, w_recv, w_send, w_update, w_msend, w_grecv, w_out,
    stage, enc_col, enc_row, dec_stage, dec_col,
    send_ext, gp, sc, rp, taken, slope, agg, normed, inv, mlat, mesh_ext,
    dcot, dsum, rcot, mc_ext, mesh_rim, lat, mcot, ucot, acot, rsum,
    scot, rim_in, acc, mgrad,
    terms, pair_in, paired, r1, s2, r2, r3, summed, gain_in, gain_held,
    load_sem, store_sem, sems, pair_sem, rs_sem, ag_sem, last_sem, gain_sem,
):
    core = lax.axis_index("dp")
    place = lax.axis_index("graph")
    twin = {"dp": 1 - core}
    left = {"graph": lax.rem(place + 63, 64)}
    right = {"graph": lax.rem(place + 1, 64)}
    coords = [lax.rem(place // stride, 4) for stride in STRIDES]

    def peer(axis, offset):
        moved = lax.rem(coords[axis] + offset, 4)
        return moved, {"graph": place + (moved - coords[axis]) * STRIDES[axis]}

    loads = {}
    for number, (name, source, target) in enumerate((
        ("w_send", w_send_any, w_send),
        ("grid", grid_any, grid_ext.at[pl.ds(GRIM, 2048)]),
        ("mesh", mesh_any, mesh),
        ("w_recv", w_recv_any, w_recv),
        ("w_grecv", w_grecv_any, w_grecv),
        ("cot", cot_any, cot),
        ("w_out", w_out_any, w_out),
        ("w_update", w_update_any, w_update),
        ("w_msend", w_msend_any, w_msend),
    )):
        loads[name] = pltpu.make_async_copy(source, target, load_sem.at[number])
        loads[name].start()

    barrier = pltpu.get_barrier_semaphore()
    targets = [left, right, twin]
    targets += [peer(axis, offset)[1] for axis in range(3) for offset in (1, 2, 3)]
    for target in targets:
        pl.semaphore_signal(
            barrier, inc=1, device_id=target, device_id_type=pl.DeviceIdType.MESH
        )
    sent = []

    def exchange(index, low, low_target, high, high_target):
        pair = [
            remote(low, low_target, sems.at[index], left),
            remote(high, high_target, sems.at[index + 1], right),
        ]
        for copy in pair:
            copy.start()
        sent.extend(pair)
        return pair

    stage[...] = jnp.zeros_like(stage)
    stage[0:KE] = enc[...] - (place * 2048 - GRIM)
    stage[KE : KE + 1] = counts[...].reshape(1, 256)
    enc_col[...] = jnp.transpose(stage[...])
    for number in range(8):
        for k in range(KE):
            enc_row[number, :, k * NODES : (k + 1) * NODES] = stage[
                k : k + 1, number * NODES : (number + 1) * NODES
            ]
    dec_stage[...] = jnp.zeros_like(dec_stage)
    dec_stage[0:3] = dec[...] - (place * 256 - MRIM)
    dec_col[...] = jnp.transpose(dec_stage[...])

    def project(start, size):
        rows = pl.ds(start, size)
        send_ext[rows] = (dot(grid_ext[rows], w_send[...]) * 0.5).astype(HALF)

    loads["w_send"].wait()
    loads["grid"].wait()
    loop(4, lambda step: project(pl.multiple_of(GRIM + step * 512, 256), 512))
    pl.semaphore_wait(barrier, 12)
    grid_halo = exchange(
        0,
        grid_ext.at[pl.ds(GRIM, GRIM)],
        grid_ext.at[pl.ds(2048 + GRIM, GRIM)],
        grid_ext.at[pl.ds(2048, GRIM)],
        grid_ext.at[pl.ds(0, GRIM)],
    )

    loads["mesh"].wait()
    loads["w_recv"].wait()
    rp[...] = dot(mesh[...], w_recv[...]).astype(HALF).astype(FULL) * 0.5
    loads["w_grecv"].wait()
    loads["cot"].wait()
    loads["w_out"].wait()

    def dense(step):
        rows = rows_at(step, 512)
        shifted = pl.ds(pl.multiple_of(GRIM + step * 512, 256), 512)
        gp[rows] = dot(grid_ext[shifted], w_grecv[...]) * 0.5
        sc[rows] = dot(cot[rows], w_out[...], ((1,), (1,))) * 0.5

    loop(4, dense)

    def encode(number):
        columns = lax.broadcasted_iota(jnp.int32, (NODES, REACH), 1) + number * (NODES * 8)
        picks = enc_col[rows_at(number, NODES)]
        selector = jnp.concatenate(
            [
                jnp.where(picks[:, k : k + 1] == columns, 1.0, 0.0).astype(HALF)
                for k in range(KE)
            ]
        )
        taken[pl.ds(0, DEPTH)] = dot(
            selector, send_ext[pl.ds(pl.multiple_of(number * (NODES * 8), 256), REACH)]
        )
        for part in range(NODES // 16):
            rows = pl.ds(pl.multiple_of(number * NODES + part * 16, 16), 16)
            number_live = enc_col[rows][:, KE : KE + 1]
            receiver = rp[rows]
            total = jnp.zeros((16, 512), FULL)
            for k in range(KE):
                at = k * NODES + part * 16
                value, bend = half_silu(taken[at : at + 16] + receiver)
                mask = jnp.where(number_live > k, 1.0, 0.0)
                total = total + value * mask
                slope[number, at : at + 16] = (bend * mask).astype(HALF)
            agg[rows] = total.astype(HALF)

    loop(7, encode, 1)
    for copy in grid_halo:
        copy.wait_recv()
    project(0, GRIM)
    project(2048 + GRIM, GRIM)
    loop(2, lambda step: encode(step * 7))

    loads["w_update"].wait()
    acot[...] = dot(agg[...], w_update[...])
    wide_gain = gain[...].astype(FULL).reshape(1, 512)

    def normalise(step):
        rows = rows_at(step, 16)
        update = acot[rows]
        scale = lax.rsqrt(jnp.mean(update * update, axis=-1, keepdims=True) + 1e-06)
        inv[rows] = jnp.broadcast_to(scale, (16, 128))
        flat = update * scale
        normed[rows] = flat
        mlat[rows] = (mesh[rows].astype(FULL) + wide_gain * flat).astype(HALF)

    loop(16, normalise)
    loads["w_msend"].wait()
    mesh_ext[pl.ds(MRIM, 256)] = (dot(mlat[...], w_msend[...]) * 0.5).astype(HALF)
    mesh_halo = exchange(
        2,
        mesh_ext.at[pl.ds(MRIM, MRIM)],
        mesh_ext.at[pl.ds(256 + MRIM, MRIM)],
        mesh_ext.at[pl.ds(256, MRIM)],
        mesh_ext.at[pl.ds(0, MRIM)],
    )
    mc_ext[...] = jnp.zeros_like(mc_ext)

    def decode(number):
        base = pl.multiple_of(number * (CELLS // 8), 64)
        cells = rows_at(number, CELLS)
        window = mesh_ext[pl.ds(base, SPAN)]
        columns = lax.broadcasted_iota(jnp.int32, (CELLS, SPAN), 1) + base
        picks = dec_col[cells]
        for j in range(3):
            selector = jnp.where(picks[:, j : j + 1] == columns, 1.0, 0.0).astype(HALF)
            taken[pl.ds(j * CELLS, CELLS)] = dot(selector, window)

        def cell_rows(step):
            inner = rows_at(step, 16)
            rows = pl.ds(pl.multiple_of(number * CELLS + step * 16, 16), 16)
            own = gp[rows]
            cotangent = sc[rows]
            total = jnp.zeros((16, 512), FULL)
            back = jnp.zeros((16, 512), FULL)
            for j in range(3):
                value, bend = half_silu(
                    taken[pl.ds(pl.multiple_of(j * CELLS + step * 16, 16), 16)] + own
                )
                total = total + value
                part = cotangent * bend
                back = back + part
                dcot[j, inner] = part.astype(HALF)
            dsum[rows] = total.astype(HALF)
            rcot[rows] = back.astype(HALF)

        lax.fori_loop(0, CELLS // 16, lambda i, c: (cell_rows(i), c)[1], 0, unroll=4)
        lines = lax.broadcasted_iota(jnp.int32, (SPAN, CELLS), 0) + base
        added = mc_ext[pl.ds(base, SPAN)]
        for j in range(3):
            line = dec_stage[j : j + 1, pl.ds(pl.multiple_of(number * CELLS, CELLS), CELLS)]
            selector = jnp.where(line == lines, 1.0, 0.0).astype(HALF)
            added = added + dot(selector, dcot[j])
        mc_ext[pl.ds(base, SPAN)] = added

    loop(3, decode, 1)
    for copy in mesh_halo:
        copy.wait_recv()
    loop(2, lambda step: decode(step * 3))
    mesh_back = exchange(
        4,
        mc_ext.at[pl.ds(0, MRIM)],
        mesh_rim.at[1],
        mc_ext.at[pl.ds(256 + MRIM, MRIM)],
        mesh_rim.at[0],
    )

    def contract(slot, lefts, rights, count, size, shift=0):
        acc[...] = jnp.zeros_like(acc)

        def piece(step):
            rows = rows_at(step, size)
            moved = pl.ds(pl.multiple_of(step * size + shift, 256), size)
            acc[...] += dot(lefts[moved], rights[rows], ((0,), (0,)))

        loop(count, piece)
        terms[slot] = acc[...].astype(HALF)

    def fan(source, target, semaphores, axis):
        copies = []
        for offset in (1, 2, 3):
            moved, device = peer(axis, offset)
            copy = remote(source(moved), target(offset), semaphores.at[offset - 1], device)
            copy.start()
            copies.append(copy)
        sent.extend(copies)
        return copies

    def everywhere(group):
        own = 2 * group + core
        copy = remote(
            terms.at[2 * group + 1 - core], pair_in.at[group], pair_sem.at[group], twin
        )
        copy.start()
        sent.append(copy)
        yield
        copy.wait_recv()
        paired[group] = (terms[own].astype(FULL) + pair_in[group].astype(FULL)).astype(HALF)
        orders = [ORDERS[(p + group) % 3] for p in range(4)]
        columns = [pl.ds(*PARTS[p]) for p in range(4)]
        waves = [
            fan(
                lambda moved: paired.at[group, rows_at(moved, 128), columns[p]],
                lambda offset: r1.at[group, offset - 1, :, columns[p]],
                rs_sem.at[4 * group + p],
                orders[p][0],
            )
            for p in range(4)
        ]
        yield
        for p in range(4):
            for copy in waves[p]:
                copy.wait_recv()
            total = paired[group, rows_at(coords[orders[p][0]], 128), columns[p]].astype(FULL)
            for slot in range(3):
                total = total + r1[group, slot, :, columns[p]].astype(FULL)
            s2[group, :, columns[p]] = total.astype(HALF)
            waves[p] = fan(
                lambda moved: s2.at[group, rows_at(moved, 32), columns[p]],
                lambda offset: r2.at[group, offset - 1, :, columns[p]],
                rs_sem.at[12 + 4 * group + p],
                orders[p][1],
            )
        yield
        for p in range(4):
            for copy in waves[p]:
                copy.wait_recv()
            total = s2[group, rows_at(coords[orders[p][1]], 32), columns[p]].astype(FULL)
            for slot in range(3):
                total = total + r2[group, slot, :, columns[p]].astype(FULL)
            mine = coords[orders[p][2]]
            r3[group, mine, :, columns[p]] = total.astype(HALF)
            waves[p] = fan(
                lambda moved: r3.at[group, mine, :, columns[p]],
                lambda offset: r3.at[group, mine, :, columns[p]],
                rs_sem.at[24 + 4 * group + p],
                orders[p][2],
            )
        yield
        for p in range(4):
            for copy in waves[p]:
                copy.wait_recv()
            total = r3[group, 0, :, columns[p]].astype(FULL)
            for slot in range(1, 4):
                total = total + r3[group, slot, :, columns[p]].astype(FULL)
            number = coords[orders[p][0]] * 4 + coords[orders[p][1]]
            rows = rows_at(number, 32)
            summed[own, rows, columns[p]] = total.astype(HALF)
            piece = summed.at[own, rows, columns[p]]
            waves[p] = fan(
                lambda moved: piece, lambda offset: piece, ag_sem.at[4 * group + p], orders[p][1]
            )
        yield
        for p in range(4):
            for copy in waves[p]:
                copy.wait_recv()
            piece = summed.at[own, rows_at(coords[orders[p][0]], 128), columns[p]]
            waves[p] = fan(
                lambda moved: piece,
                lambda offset: piece,
                ag_sem.at[12 + 4 * group + p],
                orders[p][0],
            )
        yield
        last = []
        for p in range(4):
            for copy in waves[p]:
                copy.wait_recv()
            piece = summed.at[own, :, columns[p]]
            copy = remote(piece, piece, last_sem.at[group, p], twin)
            copy.start()
            last.append(copy)
        sent.extend(last)
        yield
        for copy in last:
            copy.wait_recv()
        copy = pltpu.make_async_copy(
            summed.at[pl.ds(2 * group, 2)],
            totals.at[pl.ds(2 * group, 2)],
            store_sem.at[group],
        )
        copy.start()
        stores.append(copy)
        yield

    def gain_everywhere():
        copy = remote(gain_held.at[0, 0], gain_in, gain_sem.at[9], twin)
        copy.start()
        sent.append(copy)
        yield
        copy.wait_recv()
        total = gain_held[0, 0] + gain_in[...]
        for step in range(3):
            mine = coords[step]
            gain_held[step + 1, mine] = total
            copies = []
            for offset in (1, 2, 3):
                piece = gain_held.at[step + 1, mine]
                copy = remote(
                    piece, piece, gain_sem.at[3 * step + offset - 1], peer(step, offset)[1]
                )
                copy.start()
                copies.append(copy)
            sent.extend(copies)
            yield
            for copy in copies:
                copy.wait_recv()
            total = gain_held[step + 1, 0]
            for slot in range(1, 4):
                total = total + gain_held[step + 1, slot]
        gain_total[...] = total
        yield

    stores = []
    running = []

    def pump(*chosen):
        for chain in chosen:
            next(chain)

    contract(0, grid_ext, rcot, 4, 512, GRIM)
    contract(1, dsum, cot, 4, 512)
    first = everywhere(0)
    second = everywhere(1)
    third = everywhere(2)
    fourth = gain_everywhere()
    pump(first)

    def first_part(step):
        rows = rows_at(step, 512)
        gp[rows] = cot[rows].astype(FULL) + dot(rcot[rows], w_grecv[...], ((1,), (1,)))

    loop(4, first_part)
    for copy in mesh_back:
        copy.wait_recv()
    mcot[pl.ds(0, MRIM)] = (mc_ext[pl.ds(MRIM, MRIM)] + mesh_rim[0]).astype(HALF)
    mcot[pl.ds(MRIM, 128)] = mc_ext[pl.ds(2 * MRIM, 128)].astype(HALF)
    mcot[pl.ds(192, MRIM)] = (mc_ext[pl.ds(256, MRIM)] + mesh_rim[1]).astype(HALF)
    lat[...] = dot(mcot[...], w_msend[...], ((1,), (1,)))
    gain_held[0, 0] = jnp.zeros((8, 128), FULL)

    def unnormalise(step, total):
        rows = rows_at(step, 16)
        flat = normed[rows]
        product = lat[rows] * flat
        scaled = lat[rows] * wide_gain
        mean = jnp.mean(scaled * flat, axis=-1, keepdims=True)
        ucot[rows] = ((scaled - flat * mean) * inv[rows][:, :1]).astype(HALF)
        return total + product[:8] + product[8:]

    rowwise = lax.fori_loop(0, 16, unnormalise, jnp.zeros((8, 512), FULL))
    gain_sum = jnp.sum(rowwise, axis=0, keepdims=True)
    for part in range(4):
        gain_held[0, 0, part : part + 1, :] = gain_sum[:, 128 * part : 128 * part + 128]
    acot[...] = dot(ucot[...], w_update[...], ((1,), (1,))) * 0.5
    contract(2, agg, ucot, 1, 256)
    contract(3, mlat, mcot, 1, 256)
    pump(second, fourth, first)

    def encode_back(number):
        for part in range(NODES // 16):
            rows = pl.ds(pl.multiple_of(number * NODES + part * 16, 16), 16)
            cotangent = acot[rows]
            total = jnp.zeros((16, 512), FULL)
            for k in range(KE):
                at = k * NODES + part * 16
                piece = cotangent * slope[number, at : at + 16].astype(FULL)
                total = total + piece
                slope[number, at : at + 16] = piece.astype(HALF)
            rsum[rows] = total.astype(HALF)

    def scatter(tile, numbers):
        total = None
        for number in numbers:
            lines = lax.broadcasted_iota(jnp.int32, (256, DEPTH), 0) + tile * 256
            selector = jnp.where(enc_row[number] == lines, 1.0, 0.0).astype(HALF)
            piece = dot(selector, slope[number])
            total = piece if total is None else total + piece
        scot[rows_at(tile, 256)] = total.astype(HALF)

    loop(2, lambda step: encode_back(step * 7))
    scatter(0, (0,))
    scatter(9, (7,))
    grid_back = exchange(
        6,
        scot.at[pl.ds(0, GRIM)],
        rim_in.at[1],
        scot.at[pl.ds(2048 + GRIM, GRIM)],
        rim_in.at[0],
    )
    loop(7, encode_back, 1)
    scatter(1, (0, 1))
    scatter(8, (6, 7))
    loop(5, lambda tile: scatter(tile, (tile - 2, tile - 1, tile)), 2)
    loop(8, lambda tile: scatter(tile, (tile - 2, tile - 1, tile)), 5)
    contract(4, mesh, rsum, 1, 256)
    contract(5, grid_ext, scot, 5, 512)
    pump(third)
    mgrad[...] = (lat[...] + dot(rsum[...], w_recv[...], ((1,), (1,)))).astype(HALF)
    copy = pltpu.make_async_copy(mgrad, mesh_grad, store_sem.at[3])
    copy.start()
    stores.append(copy)
    pump(fourth, first, second, third)

    for copy in grid_back:
        copy.wait_recv()
    for rim, start in ((0, GRIM), (1, 2048)):
        rows = pl.ds(start, GRIM)
        scot[rows] = (scot[rows].astype(FULL) + rim_in[rim].astype(FULL)).astype(HALF)

    def last_part(step):
        rows = rows_at(step, 512)
        shifted = pl.ds(pl.multiple_of(GRIM + step * 512, 256), 512)
        dsum[rows] = (gp[rows] + dot(scot[shifted], w_send[...], ((1,), (1,)))).astype(HALF)

    loop(4, last_part)
    copy = pltpu.make_async_copy(dsum, grid_grad, store_sem.at[4])
    copy.start()
    stores.append(copy)
    for chain in (fourth, first, second, third) * 8:
        next(chain, None)
    for copy in sent:
        copy.wait_send()
    for copy in stores:
        copy.wait()


def everything(*operands):
    vmem = pltpu.VMEM
    anywhere = pl.BlockSpec(memory_space=pl.ANY)
    near = pl.BlockSpec(memory_space=vmem)
    return pl.pallas_call(
        whole_kernel,
        out_shape=(
            jax.ShapeDtypeStruct((2048, 512), HALF),
            jax.ShapeDtypeStruct((256, 512), HALF),
            jax.ShapeDtypeStruct((6, 512, 512), HALF),
            jax.ShapeDtypeStruct((8, 128), FULL),
        ),
        in_specs=[anywhere] * 3 + [near] * 3 + [anywhere] * 3 + [near] + [anywhere] * 3,
        out_specs=[anywhere, anywhere, anywhere, near],
        scratch_shapes=[
            vmem((2048 + 2 * GRIM, 512), HALF),
            vmem((256, 512), HALF),
            vmem((2048, 512), HALF),
        ]
        + [vmem((512, 512), HALF)] * 6
        + [
            vmem((16, 256), jnp.int32),
            vmem((256, 16), jnp.int32),
            vmem((8, 1, DEPTH), jnp.int32),
            vmem((8, 2048), jnp.int32),
            vmem((2048, 8), jnp.int32),
            vmem((2048 + 2 * GRIM, 512), HALF),
            vmem((2048, 512), FULL),
            vmem((2048, 512), FULL),
            vmem((256, 512), FULL),
            vmem((3 * CELLS, 512), FULL),
            vmem((8, DEPTH, 512), HALF),
            vmem((256, 512), HALF),
            vmem((256, 512), FULL),
            vmem((256, 128), FULL),
            vmem((256, 512), HALF),
            vmem((256 + 2 * MRIM, 512), HALF),
            vmem((3, CELLS, 512), HALF),
            vmem((2048, 512), HALF),
            vmem((2048, 512), HALF),
            vmem((256 + 2 * MRIM, 512), FULL),
            vmem((2, MRIM, 512), FULL),
            vmem((256, 512), FULL),
            vmem((256, 512), HALF),
            vmem((256, 512), HALF),
            vmem((256, 512), FULL),
            vmem((256, 512), HALF),
            vmem((2048 + 2 * GRIM, 512), HALF),
            vmem((2, GRIM, 512), HALF),
            vmem((512, 512), FULL),
            vmem((256, 512), HALF),
            vmem((6, 512, 512), HALF),
            vmem((3, 512, 512), HALF),
            vmem((3, 512, 512), HALF),
            vmem((3, 3, 128, 512), HALF),
            vmem((3, 128, 512), HALF),
            vmem((3, 3, 32, 512), HALF),
            vmem((3, 4, 32, 512), HALF),
            vmem((6, 512, 512), HALF),
            vmem((8, 128), FULL),
            vmem((4, 4, 8, 128), FULL),
            pltpu.SemaphoreType.DMA((9,)),
            pltpu.SemaphoreType.DMA((5,)),
            pltpu.SemaphoreType.DMA((8, 2)),
            pltpu.SemaphoreType.DMA((3, 2)),
            pltpu.SemaphoreType.DMA((36, 3, 2)),
            pltpu.SemaphoreType.DMA((24, 3, 2)),
            pltpu.SemaphoreType.DMA((3, 4, 2)),
            pltpu.SemaphoreType.DMA((10, 2)),
        ],
        compiler_params=pltpu.CompilerParams(
            collective_id=0, has_side_effects=True, vmem_limit_bytes=62 * 1024 * 1024
        ),
    )(*operands)


def finish_kernel(factor, grid_in, mesh_in, totals, gain, *rest):
    grid_out, mesh_out = rest[:2]
    outs = rest[2:8]
    gain_out, held, wide, grid_held, mesh_held, in_sem, out_sem, copy_sem = rest[8:]
    reads = []
    for slot in range(6):
        reads.append(pltpu.make_async_copy(totals.at[slot], held.at[slot], in_sem.at[slot]))
        reads[slot].start()
    near = [
        pltpu.make_async_copy(grid_in, grid_held, copy_sem.at[0]),
        pltpu.make_async_copy(mesh_in, mesh_held, copy_sem.at[1]),
    ]
    for copy in near:
        copy.start()
    copies = [
        pltpu.make_async_copy(grid_held, grid_out, copy_sem.at[2]),
        pltpu.make_async_copy(mesh_held, mesh_out, copy_sem.at[3]),
    ]
    for part in range(4):
        gain_out[128 * part : 128 * part + 128] = gain[part] * factor
    for slot in range(6):
        reads[slot].wait()
        wide[slot] = held[slot].astype(FULL) * factor
        copies.append(pltpu.make_async_copy(wide.at[slot], outs[slot], out_sem.at[slot]))
        copies[-1].start()
    for number in range(2):
        near[number].wait()
        copies[number].start()
    for copy in copies:
        copy.wait()


def finish(factor, grid_grad, mesh_grad, totals, gain_total):
    vmem = pltpu.VMEM
    anywhere = pl.BlockSpec(memory_space=pl.ANY)
    near = pl.BlockSpec(memory_space=vmem)
    return pl.pallas_call(
        functools.partial(finish_kernel, factor),
        out_shape=[
            jax.ShapeDtypeStruct((2048, 512), HALF),
            jax.ShapeDtypeStruct((256, 512), HALF),
        ]
        + [jax.ShapeDtypeStruct((512, 512), FULL)] * 6
        + [jax.ShapeDtypeStruct((512,), FULL)],
        in_specs=[anywhere] * 3 + [near],
        out_specs=[anywhere] * 8 + [near],
        scratch_shapes=[
            vmem((6, 512, 512), HALF),
            vmem((6, 512, 512), FULL),
            vmem((2048, 512), HALF),
            vmem((256, 512), HALF),
            pltpu.SemaphoreType.DMA((6,)),
            pltpu.SemaphoreType.DMA((6,)),
            pltpu.SemaphoreType.DMA((4,)),
        ],
        compiler_params=pltpu.CompilerParams(vmem_limit_bytes=62 * 1024 * 1024),
    )(grid_grad, mesh_grad, totals, gain_total)


def shards(
    grid_latent,
    mesh_init,
    cotangent,
    enc_senders,
    enc_counts,
    dec_senders,
    recv_weight,
    send_weight,
    update_weight,
    norm_gain,
    mesh_send_weight,
    grid_recv_weight,
    output_weight,
):
    grid_grad, mesh_grad, totals, gain_total = everything(
        grid_latent[0],
        mesh_init[0],
        cotangent[0],
        enc_senders,
        enc_counts,
        dec_senders,
        recv_weight,
        send_weight,
        update_weight,
        norm_gain,
        mesh_send_weight,
        grid_recv_weight,
        output_weight,
    )
    factor = 1.0 / math.sqrt(2048 * lax.axis_size("graph") * lax.axis_size("dp"))
    outs = finish(factor, grid_grad, mesh_grad, totals, gain_total)
    order = (6, 7, 4, 8, 5, 2, 3)
    return (outs[0][None], outs[1][None]) + tuple(outs[number] for number in order)


def solution(mesh):
    return jax.shard_map(
        shards,
        mesh=mesh,
        in_specs=(
            P("dp", "graph", None),
            P("dp", "graph", None),
            P("dp", "graph", None),
            P(None, "graph"),
            P("graph"),
            P(None, "graph"),
            P(),
            P(),
            P(),
            P(),
            P(),
            P(),
            P(),
        ),
        out_specs=(
            P("dp", "graph", None),
            P("dp", "graph", None),
            P(),
            P(),
            P(),
            P(),
            P(),
            P(),
            P(),
        ),
        check_vma=False,
    )
```

```python
import functools
import math

import jax
import jax.numpy as jnp
from jax import lax
from jax.experimental import pallas as pl
from jax.experimental.pallas import tpu as pltpu
from jax.sharding import PartitionSpec as P

KE = 12
GRIM = 256
MRIM = 64


STRIDES = (16, 4, 1)
ORDERS = ((0, 1, 2), (1, 2, 0), (2, 0, 1))


def remote(src, dst, sems, target):
    return pltpu.make_async_remote_copy(
        src_ref=src,
        dst_ref=dst,
        send_sem=sems.at[0],
        recv_sem=sems.at[1],
        device_id=target,
        device_id_type=pl.DeviceIdType.MESH,
    )


HALF = jnp.bfloat16
FULL = jnp.float32
NODES = 32
DEPTH = KE * NODES
REACH = NODES * 8 + 2 * GRIM
CELLS = 512
SPAN = CELLS // 8 + 2 * MRIM
PARTS = ((0, 128), (128, 128), (256, 128), (384, 128))


def dot(left, right, dims=((1,), (0,))):
    return lax.dot_general(left, right, (dims, ((), ())), preferred_element_type=FULL)


def loop(count, body, start=0):
    lax.fori_loop(start, count, lambda step, carry: (body(step), carry)[1], 0)


def rows_at(index, size):
    return pl.ds(pl.multiple_of(index * size, size), size)


def slope_rows(number, at):
    return pl.ds(pl.multiple_of(number * DEPTH + at, 16), 16)


def half_silu(half_pre):
    bend = jnp.tanh(half_pre)
    lifted = 1.0 + bend
    value = half_pre * lifted
    return value, lifted + value * (1.0 - bend)


def whole_kernel(
    grid_any, mesh_any, cot_any, enc_any, counts_any, dec_any,
    w_recv_any, w_send_any, w_update_any, gain_any, w_msend_any, w_grecv_any, w_out_any,
    grid_grad, mesh_grad, totals, gain_total,
    grid_ext, mesh, cot, w_recv, w_send, w_update, w_msend, w_grecv, w_out,
    enc, counts, dec, gain, stage, enc_col, enc_row, dec_stage, dec_col,
    send_ext, gp, sc, rp, taken, slope, agg, normed, inv, mlat, mesh_ext,
    dcot, dsum, rcot, mc_ext, mesh_rim, lat, mcot, ucot, acot, rsum,
    scot, rim_in, acc, mgrad,
    terms, pair_in, paired, r1, s2, r2, r3, summed, gain_in, gain_held,
    load_sem, store_sem, sems, pair_sem, rs_sem, ag_sem, last_sem, gain_sem,
):
    core = lax.axis_index("dp")
    place = lax.axis_index("graph")
    twin = {"dp": 1 - core}
    left = {"graph": lax.rem(place + 63, 64)}
    right = {"graph": lax.rem(place + 1, 64)}
    coords = [lax.rem(place // stride, 4) for stride in STRIDES]

    def peer(axis, offset):
        moved = lax.rem(coords[axis] + offset, 4)
        return moved, {"graph": place + (moved - coords[axis]) * STRIDES[axis]}

    loads = {}
    for number, (name, source, target) in enumerate((
        ("w_send", w_send_any, w_send),
        ("grid", grid_any, grid_ext.at[pl.ds(GRIM, 2048)]),
        ("enc", enc_any, enc),
        ("counts", counts_any, counts),
        ("dec", dec_any, dec),
        ("mesh", mesh_any, mesh),
        ("w_recv", w_recv_any, w_recv),
        ("w_grecv", w_grecv_any, w_grecv),
        ("cot", cot_any, cot),
        ("w_out", w_out_any, w_out),
        ("gain", gain_any, gain),
        ("w_update", w_update_any, w_update),
        ("w_msend", w_msend_any, w_msend),
    )):
        loads[name] = pltpu.make_async_copy(source, target, load_sem.at[number])
        loads[name].start()

    barrier = pltpu.get_barrier_semaphore()
    targets = [left, right, twin]
    targets += [peer(axis, offset)[1] for axis in range(3) for offset in (1, 2, 3)]
    for target in targets:
        pl.semaphore_signal(
            barrier, inc=1, device_id=target, device_id_type=pl.DeviceIdType.MESH
        )
    sent = []

    def exchange(index, low, low_target, high, high_target):
        pair = [
            remote(low, low_target, sems.at[index], left),
            remote(high, high_target, sems.at[index + 1], right),
        ]
        for copy in pair:
            copy.start()
        sent.extend(pair)
        return pair

    pl.semaphore_wait(barrier, 12)
    grid_halo = exchange(
        0,
        grid_any.at[pl.ds(0, GRIM)],
        grid_ext.at[pl.ds(2048 + GRIM, GRIM)],
        grid_any.at[pl.ds(2048 - GRIM, GRIM)],
        grid_ext.at[pl.ds(0, GRIM)],
    )

    def project(start, size):
        rows = pl.ds(start, size)
        send_ext[rows] = (dot(grid_ext[rows], w_send[...]) * 0.5).astype(HALF)

    loads["w_send"].wait()
    loads["grid"].wait()
    loop(4, lambda step: project(pl.multiple_of(GRIM + step * 512, 256), 512))
    for name in ("enc", "counts", "dec"):
        loads[name].wait()
    stage[...] = jnp.zeros_like(stage)
    stage[0:KE] = enc[...] - (place * 2048 - GRIM)
    stage[KE : KE + 1] = counts[...].reshape(1, 256)
    enc_col[...] = jnp.transpose(stage[...])
    for number in range(8):
        for k in range(KE):
            at = number * DEPTH + k * NODES
            enc_row[:, at : at + NODES] = stage[
                k : k + 1, number * NODES : (number + 1) * NODES
            ]
    dec_stage[...] = jnp.zeros_like(dec_stage)
    dec_stage[0:3] = dec[...] - (place * 256 - MRIM)
    dec_col[...] = jnp.transpose(dec_stage[...])

    loads["mesh"].wait()
    loads["w_recv"].wait()
    rp[...] = dot(mesh[...], w_recv[...]).astype(HALF).astype(FULL) * 0.5
    loads["w_grecv"].wait()
    loads["cot"].wait()
    loads["w_out"].wait()

    def dense(step):
        rows = rows_at(step, 512)
        shifted = pl.ds(pl.multiple_of(GRIM + step * 512, 256), 512)
        gp[rows] = dot(grid_ext[shifted], w_grecv[...]) * 0.5
        sc[rows] = dot(cot[rows], w_out[...], ((1,), (1,))) * 0.5

    loop(4, dense)

    def encode(number):
        columns = lax.broadcasted_iota(jnp.int32, (NODES, REACH), 1) + number * (NODES * 8)
        picks = enc_col[rows_at(number, NODES)]
        selector = jnp.concatenate(
            [
                jnp.where(picks[:, k : k + 1] == columns, 1.0, 0.0).astype(HALF)
                for k in range(KE)
            ]
        )
        taken[pl.ds(0, DEPTH)] = dot(
            selector, send_ext[pl.ds(pl.multiple_of(number * (NODES * 8), 256), REACH)]
        )
        for part in range(NODES // 16):
            rows = pl.ds(pl.multiple_of(number * NODES + part * 16, 16), 16)
            number_live = enc_col[rows][:, KE : KE + 1]
            receiver = rp[rows]
            total = jnp.zeros((16, 512), FULL)
            for k in range(KE):
                at = k * NODES + part * 16
                value, bend = half_silu(taken[at : at + 16] + receiver)
                mask = jnp.where(number_live > k, 1.0, 0.0)
                total = total + value * mask
                slope[slope_rows(number, at)] = (bend * mask).astype(HALF)
            agg[rows] = total.astype(HALF)

    loop(7, encode, 1)
    for copy in grid_halo:
        copy.wait_recv()
    project(0, GRIM)
    project(2048 + GRIM, GRIM)
    loop(2, lambda step: encode(step * 7))

    loads["w_update"].wait()
    acot[...] = dot(agg[...], w_update[...])
    loads["gain"].wait()
    wide_gain = gain[...].astype(FULL).reshape(1, 512)

    def normalise(step):
        rows = rows_at(step, 16)
        update = acot[rows]
        scale = lax.rsqrt(jnp.mean(update * update, axis=-1, keepdims=True) + 1e-06)
        inv[rows] = jnp.broadcast_to(scale, (16, 128))
        flat = update * scale
        normed[rows] = flat
        mlat[rows] = (mesh[rows].astype(FULL) + wide_gain * flat).astype(HALF)

    loop(16, normalise)
    loads["w_msend"].wait()
    mesh_ext[pl.ds(MRIM, 256)] = (dot(mlat[...], w_msend[...]) * 0.5).astype(HALF)
    mesh_halo = exchange(
        2,
        mesh_ext.at[pl.ds(MRIM, MRIM)],
        mesh_ext.at[pl.ds(256 + MRIM, MRIM)],
        mesh_ext.at[pl.ds(256, MRIM)],
        mesh_ext.at[pl.ds(0, MRIM)],
    )
    mc_ext[...] = jnp.zeros_like(mc_ext)

    def decode(number):
        base = pl.multiple_of(number * (CELLS // 8), 64)
        cells = rows_at(number, CELLS)
        window = mesh_ext[pl.ds(base, SPAN)]
        columns = lax.broadcasted_iota(jnp.int32, (CELLS, SPAN), 1) + base
        picks = dec_col[cells]
        for j in range(3):
            selector = jnp.where(picks[:, j : j + 1] == columns, 1.0, 0.0).astype(HALF)
            taken[pl.ds(j * CELLS, CELLS)] = dot(selector, window)

        def cell_rows(step):
            inner = rows_at(step, 16)
            rows = pl.ds(pl.multiple_of(number * CELLS + step * 16, 16), 16)
            own = gp[rows]
            cotangent = sc[rows]
            total = jnp.zeros((16, 512), FULL)
            back = jnp.zeros((16, 512), FULL)
            for j in range(3):
                value, bend = half_silu(
                    taken[pl.ds(pl.multiple_of(j * CELLS + step * 16, 16), 16)] + own
                )
                total = total + value
                part = cotangent * bend
                back = back + part
                dcot[j, inner] = part.astype(HALF)
            dsum[rows] = total.astype(HALF)
            rcot[rows] = back.astype(HALF)

        lax.fori_loop(0, CELLS // 16, lambda i, c: (cell_rows(i), c)[1], 0, unroll=4)
        lines = lax.broadcasted_iota(jnp.int32, (SPAN, CELLS), 0) + base
        added = mc_ext[pl.ds(base, SPAN)]
        for j in range(3):
            line = dec_stage[j : j + 1, pl.ds(pl.multiple_of(number * CELLS, CELLS), CELLS)]
            selector = jnp.where(line == lines, 1.0, 0.0).astype(HALF)
            added = added + dot(selector, dcot[j])
        mc_ext[pl.ds(base, SPAN)] = added

    loop(3, decode, 1)
    for copy in mesh_halo:
        copy.wait_recv()
    loop(2, lambda step: decode(step * 3))
    mesh_back = exchange(
        4,
        mc_ext.at[pl.ds(0, MRIM)],
        mesh_rim.at[1],
        mc_ext.at[pl.ds(256 + MRIM, MRIM)],
        mesh_rim.at[0],
    )

    def contract(slot, lefts, rights, count, size, shift=0):
        acc[...] = jnp.zeros_like(acc)

        def piece(step):
            rows = rows_at(step, size)
            moved = pl.ds(pl.multiple_of(step * size + shift, 256), size)
            acc[...] += dot(lefts[moved], rights[rows], ((0,), (0,)))

        loop(count, piece)
        terms[slot] = acc[...].astype(HALF)

    def fan(source, target, semaphores, axis):
        copies = []
        for offset in (1, 2, 3):
            moved, device = peer(axis, offset)
            copy = remote(source(moved), target(offset), semaphores.at[offset - 1], device)
            copy.start()
            copies.append(copy)
        sent.extend(copies)
        return copies

    def everywhere(group):
        own = 2 * group + core
        halves = []
        for half in range(2):
            part = pl.ds(256 * half, 256)
            copy = remote(
                terms.at[2 * group + 1 - core, :, part],
                pair_in.at[group, :, part],
                pair_sem.at[group, half],
                twin,
            )
            copy.start()
            halves.append(copy)
            if group == 2 and half == 0:
                yield
        sent.extend(halves)
        yield
        orders = [ORDERS[(p + group) % 3] for p in range(4)]
        columns = [pl.ds(*PARTS[p]) for p in range(4)]
        waves = []
        for half in range(2):
            halves[half].wait_recv()
            part = pl.ds(256 * half, 256)

            def pair_rows(step):
                rows = rows_at(step, 64)
                paired[group, rows, part] = (
                    terms[own, rows, part].astype(FULL) + pair_in[group, rows, part].astype(FULL)
                ).astype(HALF)

            loop(8, pair_rows)
            for p in (2 * half, 2 * half + 1):
                waves.append(
                    fan(
                        lambda moved: paired.at[group, rows_at(moved, 128), columns[p]],
                        lambda offset: r1.at[group, offset - 1, :, columns[p]],
                        rs_sem.at[4 * group + p],
                        orders[p][0],
                    )
                )
        yield
        for p in range(4):
            for copy in waves[p]:
                copy.wait_recv()
            total = paired[group, rows_at(coords[orders[p][0]], 128), columns[p]].astype(FULL)
            for slot in range(3):
                total = total + r1[group, slot, :, columns[p]].astype(FULL)
            s2[group, :, columns[p]] = total.astype(HALF)
            waves[p] = fan(
                lambda moved: s2.at[group, rows_at(moved, 32), columns[p]],
                lambda offset: r2.at[group, offset - 1, :, columns[p]],
                rs_sem.at[12 + 4 * group + p],
                orders[p][1],
            )
        yield
        for p in range(4):
            for copy in waves[p]:
                copy.wait_recv()
            total = s2[group, rows_at(coords[orders[p][1]], 32), columns[p]].astype(FULL)
            for slot in range(3):
                total = total + r2[group, slot, :, columns[p]].astype(FULL)
            mine = coords[orders[p][2]]
            r3[group, mine, :, columns[p]] = total.astype(HALF)
            waves[p] = fan(
                lambda moved: r3.at[group, mine, :, columns[p]],
                lambda offset: r3.at[group, mine, :, columns[p]],
                rs_sem.at[24 + 4 * group + p],
                orders[p][2],
            )
        yield
        for p in range(4):
            for copy in waves[p]:
                copy.wait_recv()
            total = r3[group, 0, :, columns[p]].astype(FULL)
            for slot in range(1, 4):
                total = total + r3[group, slot, :, columns[p]].astype(FULL)
            number = coords[orders[p][0]] * 4 + coords[orders[p][1]]
            rows = rows_at(number, 32)
            summed[own, rows, columns[p]] = total.astype(HALF)
            piece = summed.at[own, rows, columns[p]]
            waves[p] = fan(
                lambda moved: piece, lambda offset: piece, ag_sem.at[4 * group + p], orders[p][1]
            )
        yield
        for p in range(4):
            for copy in waves[p]:
                copy.wait_recv()
            piece = summed.at[own, rows_at(coords[orders[p][0]], 128), columns[p]]
            waves[p] = fan(
                lambda moved: piece,
                lambda offset: piece,
                ag_sem.at[12 + 4 * group + p],
                orders[p][0],
            )
        yield
        last = []
        for p in range(4):
            for copy in waves[p]:
                copy.wait_recv()
            piece = summed.at[own, :, columns[p]]
            copy = remote(piece, piece, last_sem.at[group, p], twin)
            copy.start()
            last.append(copy)
        sent.extend(last)
        yield
        for copy in last:
            copy.wait_recv()
        copy = pltpu.make_async_copy(
            summed.at[pl.ds(2 * group, 2)],
            totals.at[pl.ds(2 * group, 2)],
            store_sem.at[group],
        )
        copy.start()
        stores.append(copy)
        yield

    def gain_everywhere():
        copy = remote(gain_held.at[0, 0], gain_in, gain_sem.at[9], twin)
        copy.start()
        sent.append(copy)
        yield
        copy.wait_recv()
        total = gain_held[0, 0] + gain_in[...]
        for step in range(3):
            mine = coords[step]
            gain_held[step + 1, mine] = total
            copies = []
            for offset in (1, 2, 3):
                piece = gain_held.at[step + 1, mine]
                copy = remote(
                    piece, piece, gain_sem.at[3 * step + offset - 1], peer(step, offset)[1]
                )
                copy.start()
                copies.append(copy)
            sent.extend(copies)
            yield
            for copy in copies:
                copy.wait_recv()
            total = gain_held[step + 1, 0]
            for slot in range(1, 4):
                total = total + gain_held[step + 1, slot]
        gain_total[...] = total
        yield

    stores = []
    running = []

    def pump(*chosen):
        for chain in chosen:
            next(chain)

    contract(0, grid_ext, rcot, 4, 512, GRIM)
    contract(1, dsum, cot, 4, 512)
    first = everywhere(0)
    second = everywhere(1)
    third = everywhere(2)
    fourth = gain_everywhere()
    pump(first)

    def first_part(step):
        rows = rows_at(step, 512)
        gp[rows] = cot[rows].astype(FULL) + dot(rcot[rows], w_grecv[...], ((1,), (1,)))

    loop(4, first_part)
    for copy in mesh_back:
        copy.wait_recv()
    mcot[pl.ds(0, MRIM)] = (mc_ext[pl.ds(MRIM, MRIM)] + mesh_rim[0]).astype(HALF)
    mcot[pl.ds(MRIM, 128)] = mc_ext[pl.ds(2 * MRIM, 128)].astype(HALF)
    mcot[pl.ds(192, MRIM)] = (mc_ext[pl.ds(256, MRIM)] + mesh_rim[1]).astype(HALF)
    lat[...] = dot(mcot[...], w_msend[...], ((1,), (1,)))
    gain_held[0, 0] = jnp.zeros((8, 128), FULL)

    def unnormalise(step, total):
        rows = rows_at(step, 16)
        flat = normed[rows]
        product = lat[rows] * flat
        scaled = lat[rows] * wide_gain
        mean = jnp.mean(scaled * flat, axis=-1, keepdims=True)
        ucot[rows] = ((scaled - flat * mean) * inv[rows][:, :1]).astype(HALF)
        return total + product[:8] + product[8:]

    rowwise = lax.fori_loop(0, 16, unnormalise, jnp.zeros((8, 512), FULL))
    gain_sum = jnp.sum(rowwise, axis=0, keepdims=True)
    for part in range(4):
        gain_held[0, 0, part : part + 1, :] = gain_sum[:, 128 * part : 128 * part + 128]
    acot[...] = dot(ucot[...], w_update[...], ((1,), (1,))) * 0.5
    contract(2, agg, ucot, 1, 256)
    contract(3, mlat, mcot, 1, 256)
    pump(second, fourth, first)

    def encode_back(number):
        for part in range(NODES // 16):
            rows = pl.ds(pl.multiple_of(number * NODES + part * 16, 16), 16)
            cotangent = acot[rows]
            total = jnp.zeros((16, 512), FULL)
            for k in range(KE):
                at = k * NODES + part * 16
                piece = cotangent * slope[slope_rows(number, at)].astype(FULL)
                total = total + piece
                slope[slope_rows(number, at)] = piece.astype(HALF)
            rsum[rows] = total.astype(HALF)

    def scatter(tile, first_block, blocks):
        depth = blocks * DEPTH
        lines = lax.broadcasted_iota(jnp.int32, (256, depth), 0) + tile * 256
        rows = pl.ds(pl.multiple_of(first_block * DEPTH, DEPTH), depth)
        selector = jnp.where(enc_row[:, rows] == lines, 1.0, 0.0).astype(HALF)
        scot[rows_at(tile, 256)] = dot(selector, slope[rows]).astype(HALF)

    loop(2, lambda step: encode_back(step * 7))
    scatter(0, 0, 1)
    scatter(9, 7, 1)
    grid_back = exchange(
        6,
        scot.at[pl.ds(0, GRIM)],
        rim_in.at[1],
        scot.at[pl.ds(2048 + GRIM, GRIM)],
        rim_in.at[0],
    )
    loop(7, encode_back, 1)
    scatter(1, 0, 2)
    scatter(8, 6, 2)
    loop(5, lambda tile: scatter(tile, tile - 2, 3), 2)
    loop(8, lambda tile: scatter(tile, tile - 2, 3), 5)
    contract(4, mesh, rsum, 1, 256)
    for half in range(2):
        part = pl.ds(256 * half, 256)
        acc[:, part] = jnp.zeros((512, 256), FULL)

        def send_piece(step):
            rows = rows_at(step, 512)
            acc[:, part] += dot(grid_ext[rows], scot[rows, part], ((0,), (0,)))

        loop(5, send_piece)
        terms[5, :, part] = acc[:, part].astype(HALF)
        pump(third)
    mgrad[...] = (lat[...] + dot(rsum[...], w_recv[...], ((1,), (1,)))).astype(HALF)
    copy = pltpu.make_async_copy(mgrad, mesh_grad, store_sem.at[3])
    copy.start()
    stores.append(copy)
    pump(fourth, first, second, third)

    for copy in grid_back:
        copy.wait_recv()
    for rim, start in ((0, GRIM), (1, 2048)):
        rows = pl.ds(start, GRIM)
        scot[rows] = (scot[rows].astype(FULL) + rim_in[rim].astype(FULL)).astype(HALF)

    def last_part(step):
        rows = rows_at(step, 512)
        shifted = pl.ds(pl.multiple_of(GRIM + step * 512, 256), 512)
        dsum[rows] = (gp[rows] + dot(scot[shifted], w_send[...], ((1,), (1,)))).astype(HALF)

    loop(4, last_part)
    copy = pltpu.make_async_copy(dsum, grid_grad, store_sem.at[4])
    copy.start()
    stores.append(copy)
    for chain in (fourth, first, second, third) * 8:
        next(chain, None)
    for copy in sent:
        copy.wait_send()
    for copy in stores:
        copy.wait()


def everything(*operands):
    vmem = pltpu.VMEM
    anywhere = pl.BlockSpec(memory_space=pl.ANY)
    near = pl.BlockSpec(memory_space=vmem)
    return pl.pallas_call(
        whole_kernel,
        out_shape=(
            jax.ShapeDtypeStruct((2048, 512), HALF),
            jax.ShapeDtypeStruct((256, 512), HALF),
            jax.ShapeDtypeStruct((6, 512, 512), HALF),
            jax.ShapeDtypeStruct((8, 128), FULL),
        ),
        in_specs=[anywhere] * len(operands),
        out_specs=[anywhere, anywhere, anywhere, near],
        scratch_shapes=[
            vmem((2048 + 2 * GRIM, 512), HALF),
            vmem((256, 512), HALF),
            vmem((2048, 512), HALF),
        ]
        + [vmem((512, 512), HALF)] * 6
        + [
            vmem((KE, 256), jnp.int32),
            vmem((256,), jnp.int32),
            vmem((3, 2048), jnp.int32),
            vmem((512,), HALF),
            vmem((16, 256), jnp.int32),
            vmem((256, 16), jnp.int32),
            vmem((1, 8 * DEPTH), jnp.int32),
            vmem((8, 2048), jnp.int32),
            vmem((2048, 8), jnp.int32),
            vmem((2048 + 2 * GRIM, 512), HALF),
            vmem((2048, 512), FULL),
            vmem((2048, 512), FULL),
            vmem((256, 512), FULL),
            vmem((3 * CELLS, 512), FULL),
            vmem((8 * DEPTH, 512), HALF),
            vmem((256, 512), HALF),
            vmem((256, 512), FULL),
            vmem((256, 128), FULL),
            vmem((256, 512), HALF),
            vmem((256 + 2 * MRIM, 512), HALF),
            vmem((3, CELLS, 512), HALF),
            vmem((2048, 512), HALF),
            vmem((2048, 512), HALF),
            vmem((256 + 2 * MRIM, 512), FULL),
            vmem((2, MRIM, 512), FULL),
            vmem((256, 512), FULL),
            vmem((256, 512), HALF),
            vmem((256, 512), HALF),
            vmem((256, 512), FULL),
            vmem((256, 512), HALF),
            vmem((2048 + 2 * GRIM, 512), HALF),
            vmem((2, GRIM, 512), HALF),
            vmem((512, 512), FULL),
            vmem((256, 512), HALF),
            vmem((6, 512, 512), HALF),
            vmem((3, 512, 512), HALF),
            vmem((3, 512, 512), HALF),
            vmem((3, 3, 128, 512), HALF),
            vmem((3, 128, 512), HALF),
            vmem((3, 3, 32, 512), HALF),
            vmem((3, 4, 32, 512), HALF),
            vmem((6, 512, 512), HALF),
            vmem((8, 128), FULL),
            vmem((4, 4, 8, 128), FULL),
            pltpu.SemaphoreType.DMA((13,)),
            pltpu.SemaphoreType.DMA((5,)),
            pltpu.SemaphoreType.DMA((8, 2)),
            pltpu.SemaphoreType.DMA((3, 2, 2)),
            pltpu.SemaphoreType.DMA((36, 3, 2)),
            pltpu.SemaphoreType.DMA((24, 3, 2)),
            pltpu.SemaphoreType.DMA((3, 4, 2)),
            pltpu.SemaphoreType.DMA((10, 2)),
        ],
        compiler_params=pltpu.CompilerParams(
            collective_id=0, has_side_effects=True, vmem_limit_bytes=62 * 1024 * 1024
        ),
    )(*operands)


def finish_kernel(factor, grid_in, mesh_in, totals, gain, *rest):
    grid_out, mesh_out = rest[:2]
    outs = rest[2:8]
    gain_out, held, wide, grid_held, mesh_held, in_sem, out_sem, copy_sem = rest[8:]
    near = [
        pltpu.make_async_copy(grid_in, grid_held, copy_sem.at[0]),
        pltpu.make_async_copy(mesh_in, mesh_held, copy_sem.at[1]),
    ]
    reads = [
        pltpu.make_async_copy(totals.at[slot], held.at[slot], in_sem.at[slot])
        for slot in range(6)
    ]
    for copy in reads[:2] + near + reads[2:]:
        copy.start()
    copies = [
        pltpu.make_async_copy(grid_held, grid_out, copy_sem.at[2]),
        pltpu.make_async_copy(mesh_held, mesh_out, copy_sem.at[3]),
    ]
    for slot in range(6):
        reads[slot].wait()

        def widen(step):
            rows = rows_at(step, 64)
            wide[slot, rows] = held[slot, rows].astype(FULL) * factor

        loop(8, widen)
        copies.append(pltpu.make_async_copy(wide.at[slot], outs[slot], out_sem.at[slot]))
        copies[-1].start()
        if slot == 1:
            for number in range(2):
                near[number].wait()
                copies[number].start()
    for part in range(4):
        gain_out[128 * part : 128 * part + 128] = gain[part] * factor
    for copy in copies:
        copy.wait()


def finish(factor, grid_grad, mesh_grad, totals, gain_total):
    vmem = pltpu.VMEM
    anywhere = pl.BlockSpec(memory_space=pl.ANY)
    near = pl.BlockSpec(memory_space=vmem)
    return pl.pallas_call(
        functools.partial(finish_kernel, factor),
        out_shape=[
            jax.ShapeDtypeStruct((2048, 512), HALF),
            jax.ShapeDtypeStruct((256, 512), HALF),
        ]
        + [jax.ShapeDtypeStruct((512, 512), FULL)] * 6
        + [jax.ShapeDtypeStruct((512,), FULL)],
        in_specs=[anywhere] * 3 + [near],
        out_specs=[anywhere] * 8 + [near],
        scratch_shapes=[
            vmem((6, 512, 512), HALF),
            vmem((6, 512, 512), FULL),
            vmem((2048, 512), HALF),
            vmem((256, 512), HALF),
            pltpu.SemaphoreType.DMA((6,)),
            pltpu.SemaphoreType.DMA((6,)),
            pltpu.SemaphoreType.DMA((4,)),
        ],
        compiler_params=pltpu.CompilerParams(vmem_limit_bytes=62 * 1024 * 1024),
    )(grid_grad, mesh_grad, totals, gain_total)


def shards(
    grid_latent,
    mesh_init,
    cotangent,
    enc_senders,
    enc_counts,
    dec_senders,
    recv_weight,
    send_weight,
    update_weight,
    norm_gain,
    mesh_send_weight,
    grid_recv_weight,
    output_weight,
):
    grid_grad, mesh_grad, totals, gain_total = everything(
        grid_latent[0],
        mesh_init[0],
        cotangent[0],
        enc_senders,
        enc_counts,
        dec_senders,
        recv_weight,
        send_weight,
        update_weight,
        norm_gain,
        mesh_send_weight,
        grid_recv_weight,
        output_weight,
    )
    factor = 1.0 / math.sqrt(2048 * lax.axis_size("graph") * lax.axis_size("dp"))
    outs = finish(factor, grid_grad, mesh_grad, totals, gain_total)
    order = (6, 7, 4, 8, 5, 2, 3)
    return (outs[0][None], outs[1][None]) + tuple(outs[number] for number in order)


def solution(mesh):
    return jax.shard_map(
        shards,
        mesh=mesh,
        in_specs=(
            P("dp", "graph", None),
            P("dp", "graph", None),
            P("dp", "graph", None),
            P(None, "graph"),
            P("graph"),
            P(None, "graph"),
            P(),
            P(),
            P(),
            P(),
            P(),
            P(),
            P(),
        ),
        out_specs=(
            P("dp", "graph", None),
            P("dp", "graph", None),
            P(),
            P(),
            P(),
            P(),
            P(),
            P(),
            P(),
        ),
        check_vma=False,
    )
```

```python
import functools
import math

import jax
import jax.numpy as jnp
from jax import lax
from jax.experimental import pallas as pl
from jax.experimental.pallas import tpu as pltpu
from jax.sharding import PartitionSpec as P

KE = 12
GRIM = 256
MRIM = 64


STRIDES = (16, 4, 1)
ORDERS = ((0, 1, 2), (1, 2, 0), (2, 0, 1))


def remote(src, dst, sems, target):
    return pltpu.make_async_remote_copy(
        src_ref=src,
        dst_ref=dst,
        send_sem=sems.at[0],
        recv_sem=sems.at[1],
        device_id=target,
        device_id_type=pl.DeviceIdType.MESH,
    )


HALF = jnp.bfloat16
FULL = jnp.float32
NODES = 32
DEPTH = KE * NODES
REACH = NODES * 8 + 2 * GRIM
CELLS = 512
SPAN = CELLS // 8 + 2 * MRIM
PARTS = ((0, 128), (128, 128), (256, 128), (384, 128))


def dot(left, right, dims=((1,), (0,))):
    return lax.dot_general(left, right, (dims, ((), ())), preferred_element_type=FULL)


def loop(count, body, start=0):
    lax.fori_loop(start, count, lambda step, carry: (body(step), carry)[1], 0)


def rows_at(index, size):
    return pl.ds(pl.multiple_of(index * size, size), size)


def slope_rows(number, at):
    return pl.ds(pl.multiple_of(number * DEPTH + at, 16), 16)


def half_silu(half_pre):
    bend = jnp.tanh(half_pre)
    lifted = 1.0 + bend
    value = half_pre * lifted
    return value, lifted + value * (1.0 - bend)


def whole_kernel(
    grid_any, mesh_any, cot_any, enc_any, counts_any, dec_any,
    w_recv_any, w_send_any, w_update_any, gain_any, w_msend_any, w_grecv_any, w_out_any,
    grid_grad, mesh_grad, totals, gain_total,
    grid_ext, mesh, cot, w_recv, w_send, w_update, w_msend, w_grecv, w_out,
    enc, counts, dec, gain, stage, enc_col, enc_row, dec_stage, dec_col,
    send_ext, gp, sc, rp, taken, slope, agg, normed, inv, mlat, mesh_ext,
    dcot, dsum, rcot, mc_ext, mesh_rim, lat, mcot, ucot, acot, rsum,
    scot, rim_in, acc, mgrad,
    terms, pair_in, paired, r1, s2, r2, r3, summed, gain_in, gain_held,
    load_sem, store_sem, sems, pair_sem, rs_sem, ag_sem, last_sem, gain_sem,
):
    core = lax.axis_index("dp")
    place = lax.axis_index("graph")
    twin = {"dp": 1 - core}
    left = {"graph": lax.rem(place + 63, 64)}
    right = {"graph": lax.rem(place + 1, 64)}
    coords = [lax.rem(place // stride, 4) for stride in STRIDES]

    def peer(axis, offset):
        moved = lax.rem(coords[axis] + offset, 4)
        return moved, {"graph": place + (moved - coords[axis]) * STRIDES[axis]}

    barrier = pltpu.get_barrier_semaphore()
    targets = [left, right, twin]
    targets += [peer(axis, offset)[1] for axis in range(3) for offset in (1, 2, 3)]
    for target in targets:
        pl.semaphore_signal(
            barrier, inc=1, device_id=target, device_id_type=pl.DeviceIdType.MESH
        )
    loads = {}
    for number, (name, source, target) in enumerate((
        ("w_send", w_send_any, w_send),
        ("grid", grid_any, grid_ext.at[pl.ds(GRIM, 2048)]),
        ("enc", enc_any, enc),
        ("counts", counts_any, counts),
        ("dec", dec_any, dec),
        ("mesh", mesh_any, mesh),
        ("w_recv", w_recv_any, w_recv),
        ("w_grecv", w_grecv_any, w_grecv),
        ("cot", cot_any, cot),
        ("w_out", w_out_any, w_out),
        ("gain", gain_any, gain),
        ("w_update", w_update_any, w_update),
        ("w_msend", w_msend_any, w_msend),
    )):
        loads[name] = pltpu.make_async_copy(source, target, load_sem.at[number])
        loads[name].start()

    sent = []

    def exchange(index, low, low_target, high, high_target):
        pair = [
            remote(low, low_target, sems.at[index], left),
            remote(high, high_target, sems.at[index + 1], right),
        ]
        for copy in pair:
            copy.start()
        sent.extend(pair)
        return pair

    pl.semaphore_wait(barrier, 12)
    grid_halo = exchange(
        0,
        grid_any.at[pl.ds(0, GRIM)],
        grid_ext.at[pl.ds(2048 + GRIM, GRIM)],
        grid_any.at[pl.ds(2048 - GRIM, GRIM)],
        grid_ext.at[pl.ds(0, GRIM)],
    )

    def project(start, size):
        rows = pl.ds(start, size)
        send_ext[rows] = (dot(grid_ext[rows], w_send[...]) * 0.5).astype(HALF)

    loads["w_send"].wait()
    loads["grid"].wait()
    loop(4, lambda step: project(pl.multiple_of(GRIM + step * 512, 256), 512))
    for name in ("enc", "counts", "dec"):
        loads[name].wait()
    stage[...] = jnp.zeros_like(stage)
    stage[0:KE] = enc[...] - (place * 2048 - GRIM)
    stage[KE : KE + 1] = counts[...].reshape(1, 256)
    enc_col[...] = jnp.transpose(stage[...])
    for number in range(8):
        for k in range(KE):
            at = number * DEPTH + k * NODES
            enc_row[:, at : at + NODES] = stage[
                k : k + 1, number * NODES : (number + 1) * NODES
            ]
    dec_stage[...] = jnp.zeros_like(dec_stage)
    dec_stage[0:3] = dec[...] - (place * 256 - MRIM)
    dec_col[...] = jnp.transpose(dec_stage[...])

    loads["mesh"].wait()
    loads["w_recv"].wait()
    rp[...] = dot(mesh[...], w_recv[...]).astype(HALF).astype(FULL) * 0.5
    loads["w_grecv"].wait()
    loads["cot"].wait()
    loads["w_out"].wait()

    def dense(step):
        rows = rows_at(step, 512)
        shifted = pl.ds(pl.multiple_of(GRIM + step * 512, 256), 512)
        gp[rows] = dot(grid_ext[shifted], w_grecv[...]) * 0.5
        sc[rows] = dot(cot[rows], w_out[...], ((1,), (1,))) * 0.5

    loop(4, dense)

    def encode(number):
        columns = lax.broadcasted_iota(jnp.int32, (NODES, REACH), 1) + number * (NODES * 8)
        picks = enc_col[rows_at(number, NODES)]
        selector = jnp.concatenate(
            [
                jnp.where(picks[:, k : k + 1] == columns, 1.0, 0.0).astype(HALF)
                for k in range(KE)
            ]
        )
        taken[pl.ds(0, DEPTH)] = dot(
            selector, send_ext[pl.ds(pl.multiple_of(number * (NODES * 8), 256), REACH)]
        )
        for part in range(NODES // 16):
            rows = pl.ds(pl.multiple_of(number * NODES + part * 16, 16), 16)
            number_live = enc_col[rows][:, KE : KE + 1]
            receiver = rp[rows]
            total = jnp.zeros((16, 512), FULL)
            for k in range(KE):
                at = k * NODES + part * 16
                value, bend = half_silu(taken[at : at + 16] + receiver)
                mask = jnp.where(number_live > k, 1.0, 0.0)
                total = total + value * mask
                slope[slope_rows(number, at)] = (bend * mask).astype(HALF)
            agg[rows] = total.astype(HALF)

    loop(7, encode, 1)
    for copy in grid_halo:
        copy.wait_recv()
    project(0, GRIM)
    project(2048 + GRIM, GRIM)
    loop(2, lambda step: encode(step * 7))

    loads["w_update"].wait()
    acot[...] = dot(agg[...], w_update[...])
    loads["gain"].wait()
    wide_gain = gain[...].astype(FULL).reshape(1, 512)

    def normalise(step):
        rows = rows_at(step, 16)
        update = acot[rows]
        scale = lax.rsqrt(jnp.mean(update * update, axis=-1, keepdims=True) + 1e-06)
        inv[rows] = jnp.broadcast_to(scale, (16, 128))
        flat = update * scale
        normed[rows] = flat
        mlat[rows] = (mesh[rows].astype(FULL) + wide_gain * flat).astype(HALF)

    loop(16, normalise)
    loads["w_msend"].wait()
    mesh_ext[pl.ds(MRIM, 256)] = (dot(mlat[...], w_msend[...]) * 0.5).astype(HALF)
    mesh_halo = exchange(
        2,
        mesh_ext.at[pl.ds(MRIM, MRIM)],
        mesh_ext.at[pl.ds(256 + MRIM, MRIM)],
        mesh_ext.at[pl.ds(256, MRIM)],
        mesh_ext.at[pl.ds(0, MRIM)],
    )
    mc_ext[...] = jnp.zeros_like(mc_ext)

    def decode(number):
        base = pl.multiple_of(number * (CELLS // 8), 64)
        cells = rows_at(number, CELLS)
        window = mesh_ext[pl.ds(base, SPAN)]
        columns = lax.broadcasted_iota(jnp.int32, (CELLS, SPAN), 1) + base
        picks = dec_col[cells]
        for j in range(3):
            selector = jnp.where(picks[:, j : j + 1] == columns, 1.0, 0.0).astype(HALF)
            taken[pl.ds(j * CELLS, CELLS)] = dot(selector, window)

        def cell_rows(step):
            inner = rows_at(step, 16)
            rows = pl.ds(pl.multiple_of(number * CELLS + step * 16, 16), 16)
            own = gp[rows]
            cotangent = sc[rows]
            total = back = None
            for j in range(3):
                value, bend = half_silu(
                    taken[pl.ds(pl.multiple_of(j * CELLS + step * 16, 16), 16)] + own
                )
                part = cotangent * bend
                total = value if j == 0 else total + value
                back = part if j == 0 else back + part
                dcot[j, inner] = part.astype(HALF)
            dsum[rows] = total.astype(HALF)
            rcot[rows] = back.astype(HALF)

        lax.fori_loop(0, CELLS // 16, lambda i, c: (cell_rows(i), c)[1], 0, unroll=4)
        lines = lax.broadcasted_iota(jnp.int32, (SPAN, CELLS), 0) + base
        added = mc_ext[pl.ds(base, SPAN)]
        for j in range(3):
            line = dec_stage[j : j + 1, pl.ds(pl.multiple_of(number * CELLS, CELLS), CELLS)]
            selector = jnp.where(line == lines, 1.0, 0.0).astype(HALF)
            added = added + dot(selector, dcot[j])
        mc_ext[pl.ds(base, SPAN)] = added

    loop(3, decode, 1)
    for copy in mesh_halo:
        copy.wait_recv()
    loop(2, lambda step: decode(step * 3))
    mesh_back = exchange(
        4,
        mc_ext.at[pl.ds(0, MRIM)],
        mesh_rim.at[1],
        mc_ext.at[pl.ds(256 + MRIM, MRIM)],
        mesh_rim.at[0],
    )

    def contract(slot, lefts, rights, count, size, shift=0):
        acc[...] = jnp.zeros_like(acc)

        def piece(step):
            rows = rows_at(step, size)
            moved = pl.ds(pl.multiple_of(step * size + shift, 256), size)
            acc[...] += dot(lefts[moved], rights[rows], ((0,), (0,)))

        loop(count, piece)
        terms[slot] = acc[...].astype(HALF)

    def fan(source, target, semaphores, axis):
        copies = []
        for offset in (1, 2, 3):
            moved, device = peer(axis, offset)
            copy = remote(source(moved), target(offset), semaphores.at[offset - 1], device)
            copy.start()
            copies.append(copy)
        sent.extend(copies)
        return copies

    def everywhere(group):
        own = 2 * group + core
        halves = []
        for half in range(2):
            part = pl.ds(256 * half, 256)
            copy = remote(
                terms.at[2 * group + 1 - core, :, part],
                pair_in.at[group, :, part],
                pair_sem.at[group, half],
                twin,
            )
            copy.start()
            halves.append(copy)
            if group == 2 and half == 0:
                yield
        sent.extend(halves)
        yield
        orders = [ORDERS[(p + group) % 3] for p in range(4)]
        columns = [pl.ds(*PARTS[p]) for p in range(4)]
        waves = []
        for half in range(2):
            halves[half].wait_recv()
            part = pl.ds(256 * half, 256)

            def pair_rows(step):
                rows = rows_at(step, 64)
                paired[group, rows, part] = (
                    terms[own, rows, part].astype(FULL) + pair_in[group, rows, part].astype(FULL)
                ).astype(HALF)

            loop(8, pair_rows)
            for p in (2 * half, 2 * half + 1):
                waves.append(
                    fan(
                        lambda moved: paired.at[group, rows_at(moved, 128), columns[p]],
                        lambda offset: r1.at[group, offset - 1, :, columns[p]],
                        rs_sem.at[4 * group + p],
                        orders[p][0],
                    )
                )
        yield
        for p in range(4):
            for copy in waves[p]:
                copy.wait_recv()
            total = paired[group, rows_at(coords[orders[p][0]], 128), columns[p]].astype(FULL)
            for slot in range(3):
                total = total + r1[group, slot, :, columns[p]].astype(FULL)
            s2[group, :, columns[p]] = total.astype(HALF)
            waves[p] = fan(
                lambda moved: s2.at[group, rows_at(moved, 32), columns[p]],
                lambda offset: r2.at[group, offset - 1, :, columns[p]],
                rs_sem.at[12 + 4 * group + p],
                orders[p][1],
            )
        yield
        for p in range(4):
            for copy in waves[p]:
                copy.wait_recv()
            total = s2[group, rows_at(coords[orders[p][1]], 32), columns[p]].astype(FULL)
            for slot in range(3):
                total = total + r2[group, slot, :, columns[p]].astype(FULL)
            mine = coords[orders[p][2]]
            r3[group, mine, :, columns[p]] = total.astype(HALF)
            waves[p] = fan(
                lambda moved: r3.at[group, mine, :, columns[p]],
                lambda offset: r3.at[group, mine, :, columns[p]],
                rs_sem.at[24 + 4 * group + p],
                orders[p][2],
            )
        yield
        for p in range(4):
            for copy in waves[p]:
                copy.wait_recv()
            total = r3[group, 0, :, columns[p]].astype(FULL)
            for slot in range(1, 4):
                total = total + r3[group, slot, :, columns[p]].astype(FULL)
            number = coords[orders[p][0]] * 4 + coords[orders[p][1]]
            rows = rows_at(number, 32)
            summed[own, rows, columns[p]] = total.astype(HALF)
            piece = summed.at[own, rows, columns[p]]
            waves[p] = fan(
                lambda moved: piece, lambda offset: piece, ag_sem.at[4 * group + p], orders[p][1]
            )
        yield
        for p in range(4):
            for copy in waves[p]:
                copy.wait_recv()
            piece = summed.at[own, rows_at(coords[orders[p][0]], 128), columns[p]]
            waves[p] = fan(
                lambda moved: piece,
                lambda offset: piece,
                ag_sem.at[12 + 4 * group + p],
                orders[p][0],
            )
        yield
        last = []
        for p in range(4):
            for copy in waves[p]:
                copy.wait_recv()
            piece = summed.at[own, :, columns[p]]
            copy = remote(piece, piece, last_sem.at[group, p], twin)
            copy.start()
            last.append(copy)
        sent.extend(last)
        yield
        for copy in last:
            copy.wait_recv()
        copy = pltpu.make_async_copy(
            summed.at[pl.ds(2 * group, 2)],
            totals.at[pl.ds(2 * group, 2)],
            store_sem.at[group],
        )
        copy.start()
        stores.append(copy)
        yield

    def gain_everywhere():
        copy = remote(gain_held.at[0, 0], gain_in, gain_sem.at[9], twin)
        copy.start()
        sent.append(copy)
        yield
        copy.wait_recv()
        total = gain_held[0, 0] + gain_in[...]
        for step in range(3):
            mine = coords[step]
            gain_held[step + 1, mine] = total
            copies = []
            for offset in (1, 2, 3):
                piece = gain_held.at[step + 1, mine]
                copy = remote(
                    piece, piece, gain_sem.at[3 * step + offset - 1], peer(step, offset)[1]
                )
                copy.start()
                copies.append(copy)
            sent.extend(copies)
            yield
            for copy in copies:
                copy.wait_recv()
            total = gain_held[step + 1, 0]
            for slot in range(1, 4):
                total = total + gain_held[step + 1, slot]
        gain_total[...] = total
        yield

    stores = []
    running = []

    def pump(*chosen):
        for chain in chosen:
            next(chain)

    contract(0, grid_ext, rcot, 4, 512, GRIM)
    contract(1, dsum, cot, 4, 512)
    first = everywhere(0)
    second = everywhere(1)
    third = everywhere(2)
    fourth = gain_everywhere()
    pump(first)

    def first_part(step):
        rows = rows_at(step, 512)
        gp[rows] = cot[rows].astype(FULL) + dot(rcot[rows], w_grecv[...], ((1,), (1,)))

    loop(4, first_part)
    for copy in mesh_back:
        copy.wait_recv()
    mcot[pl.ds(0, MRIM)] = (mc_ext[pl.ds(MRIM, MRIM)] + mesh_rim[0]).astype(HALF)
    mcot[pl.ds(MRIM, 128)] = mc_ext[pl.ds(2 * MRIM, 128)].astype(HALF)
    mcot[pl.ds(192, MRIM)] = (mc_ext[pl.ds(256, MRIM)] + mesh_rim[1]).astype(HALF)
    lat[...] = dot(mcot[...], w_msend[...], ((1,), (1,)))
    gain_held[0, 0] = jnp.zeros((8, 128), FULL)

    def unnormalise(step, total):
        rows = rows_at(step, 16)
        flat = normed[rows]
        product = lat[rows] * flat
        scaled = lat[rows] * wide_gain
        mean = jnp.mean(scaled * flat, axis=-1, keepdims=True)
        ucot[rows] = ((scaled - flat * mean) * inv[rows][:, :1]).astype(HALF)
        return total + product[:8] + product[8:]

    rowwise = lax.fori_loop(0, 16, unnormalise, jnp.zeros((8, 512), FULL))
    gain_sum = jnp.sum(rowwise, axis=0, keepdims=True)
    for part in range(4):
        gain_held[0, 0, part : part + 1, :] = gain_sum[:, 128 * part : 128 * part + 128]
    acot[...] = dot(ucot[...], w_update[...], ((1,), (1,))) * 0.5
    contract(2, agg, ucot, 1, 256)
    contract(3, mlat, mcot, 1, 256)
    pump(second, fourth, first)

    def encode_back(number):
        for part in range(NODES // 16):
            rows = pl.ds(pl.multiple_of(number * NODES + part * 16, 16), 16)
            cotangent = acot[rows]
            total = jnp.zeros((16, 512), FULL)
            for k in range(KE):
                at = k * NODES + part * 16
                piece = cotangent * slope[slope_rows(number, at)].astype(FULL)
                total = total + piece
                slope[slope_rows(number, at)] = piece.astype(HALF)
            rsum[rows] = total.astype(HALF)

    def scatter(tile, first_block, blocks):
        depth = blocks * DEPTH
        lines = lax.broadcasted_iota(jnp.int32, (256, depth), 0) + tile * 256
        rows = pl.ds(pl.multiple_of(first_block * DEPTH, DEPTH), depth)
        selector = jnp.where(enc_row[:, rows] == lines, 1.0, 0.0).astype(HALF)
        scot[rows_at(tile, 256)] = dot(selector, slope[rows]).astype(HALF)

    loop(2, lambda step: encode_back(step * 7))
    scatter(0, 0, 1)
    scatter(9, 7, 1)
    grid_back = exchange(
        6,
        scot.at[pl.ds(0, GRIM)],
        rim_in.at[1],
        scot.at[pl.ds(2048 + GRIM, GRIM)],
        rim_in.at[0],
    )
    loop(7, encode_back, 1)
    scatter(1, 0, 2)
    scatter(8, 6, 2)
    loop(5, lambda tile: scatter(tile, tile - 2, 3), 2)
    loop(8, lambda tile: scatter(tile, tile - 2, 3), 5)
    contract(4, mesh, rsum, 1, 256)
    for half in range(2):
        part = pl.ds(256 * half, 256)
        acc[:, part] = jnp.zeros((512, 256), FULL)

        def send_piece(step):
            rows = rows_at(step, 512)
            acc[:, part] += dot(grid_ext[rows], scot[rows, part], ((0,), (0,)))

        loop(5, send_piece)
        terms[5, :, part] = acc[:, part].astype(HALF)
        pump(third)
    mgrad[...] = (lat[...] + dot(rsum[...], w_recv[...], ((1,), (1,)))).astype(HALF)
    copy = pltpu.make_async_copy(mgrad, mesh_grad, store_sem.at[3])
    copy.start()
    stores.append(copy)
    pump(fourth, first, second, third)

    for copy in grid_back:
        copy.wait_recv()
    for rim, start in ((0, GRIM), (1, 2048)):
        rows = pl.ds(start, GRIM)
        scot[rows] = (scot[rows].astype(FULL) + rim_in[rim].astype(FULL)).astype(HALF)

    def last_part(step):
        rows = rows_at(step, 512)
        shifted = pl.ds(pl.multiple_of(GRIM + step * 512, 256), 512)
        dsum[rows] = (gp[rows] + dot(scot[shifted], w_send[...], ((1,), (1,)))).astype(HALF)

    loop(4, last_part)
    copy = pltpu.make_async_copy(dsum, grid_grad, store_sem.at[4])
    copy.start()
    stores.append(copy)
    for chain in (fourth, first, second, third) * 8:
        next(chain, None)
    for copy in sent:
        copy.wait_send()
    for copy in stores:
        copy.wait()


def everything(*operands):
    vmem = pltpu.VMEM
    anywhere = pl.BlockSpec(memory_space=pl.ANY)
    near = pl.BlockSpec(memory_space=vmem)
    return pl.pallas_call(
        whole_kernel,
        out_shape=(
            jax.ShapeDtypeStruct((2048, 512), HALF),
            jax.ShapeDtypeStruct((256, 512), HALF),
            jax.ShapeDtypeStruct((6, 512, 512), HALF),
            jax.ShapeDtypeStruct((8, 128), FULL),
        ),
        in_specs=[anywhere] * len(operands),
        out_specs=[anywhere, anywhere, anywhere, near],
        scratch_shapes=[
            vmem((2048 + 2 * GRIM, 512), HALF),
            vmem((256, 512), HALF),
            vmem((2048, 512), HALF),
        ]
        + [vmem((512, 512), HALF)] * 6
        + [
            vmem((KE, 256), jnp.int32),
            vmem((256,), jnp.int32),
            vmem((3, 2048), jnp.int32),
            vmem((512,), HALF),
            vmem((16, 256), jnp.int32),
            vmem((256, 16), jnp.int32),
            vmem((1, 8 * DEPTH), jnp.int32),
            vmem((8, 2048), jnp.int32),
            vmem((2048, 8), jnp.int32),
            vmem((2048 + 2 * GRIM, 512), HALF),
            vmem((2048, 512), FULL),
            vmem((2048, 512), FULL),
            vmem((256, 512), FULL),
            vmem((3 * CELLS, 512), FULL),
            vmem((8 * DEPTH, 512), HALF),
            vmem((256, 512), HALF),
            vmem((256, 512), FULL),
            vmem((256, 128), FULL),
            vmem((256, 512), HALF),
            vmem((256 + 2 * MRIM, 512), HALF),
            vmem((3, CELLS, 512), HALF),
            vmem((2048, 512), HALF),
            vmem((2048, 512), HALF),
            vmem((256 + 2 * MRIM, 512), FULL),
            vmem((2, MRIM, 512), FULL),
            vmem((256, 512), FULL),
            vmem((256, 512), HALF),
            vmem((256, 512), HALF),
            vmem((256, 512), FULL),
            vmem((256, 512), HALF),
            vmem((2048 + 2 * GRIM, 512), HALF),
            vmem((2, GRIM, 512), HALF),
            vmem((512, 512), FULL),
            vmem((256, 512), HALF),
            vmem((6, 512, 512), HALF),
            vmem((3, 512, 512), HALF),
            vmem((3, 512, 512), HALF),
            vmem((3, 3, 128, 512), HALF),
            vmem((3, 128, 512), HALF),
            vmem((3, 3, 32, 512), HALF),
            vmem((3, 4, 32, 512), HALF),
            vmem((6, 512, 512), HALF),
            vmem((8, 128), FULL),
            vmem((4, 4, 8, 128), FULL),
            pltpu.SemaphoreType.DMA((13,)),
            pltpu.SemaphoreType.DMA((5,)),
            pltpu.SemaphoreType.DMA((8, 2)),
            pltpu.SemaphoreType.DMA((3, 2, 2)),
            pltpu.SemaphoreType.DMA((36, 3, 2)),
            pltpu.SemaphoreType.DMA((24, 3, 2)),
            pltpu.SemaphoreType.DMA((3, 4, 2)),
            pltpu.SemaphoreType.DMA((10, 2)),
        ],
        compiler_params=pltpu.CompilerParams(
            collective_id=0, has_side_effects=True, vmem_limit_bytes=62 * 1024 * 1024
        ),
    )(*operands)


def finish_kernel(factor, grid_in, mesh_in, totals, gain, *rest):
    grid_out, mesh_out = rest[:2]
    outs = rest[2:8]
    gain_out, held, wide, grid_held, mesh_held, in_sem, out_sem, copy_sem = rest[8:]
    near = [
        pltpu.make_async_copy(grid_in, grid_held, copy_sem.at[0]),
        pltpu.make_async_copy(mesh_in, mesh_held, copy_sem.at[1]),
    ]
    reads = [
        pltpu.make_async_copy(totals.at[slot], held.at[slot], in_sem.at[slot])
        for slot in range(6)
    ]
    for copy in reads[:2] + near + reads[2:]:
        copy.start()
    copies = [
        pltpu.make_async_copy(grid_held, grid_out, copy_sem.at[2]),
        pltpu.make_async_copy(mesh_held, mesh_out, copy_sem.at[3]),
    ]
    for slot in range(6):
        reads[slot].wait()

        def widen(step):
            rows = rows_at(step, 64)
            wide[slot, rows] = held[slot, rows].astype(FULL) * factor

        loop(8, widen)
        copies.append(pltpu.make_async_copy(wide.at[slot], outs[slot], out_sem.at[slot]))
        copies[-1].start()
        if slot == 1:
            for number in range(2):
                near[number].wait()
                copies[number].start()
    for part in range(4):
        gain_out[128 * part : 128 * part + 128] = gain[part] * factor
    for copy in copies:
        copy.wait()


def finish(factor, grid_grad, mesh_grad, totals, gain_total):
    vmem = pltpu.VMEM
    anywhere = pl.BlockSpec(memory_space=pl.ANY)
    near = pl.BlockSpec(memory_space=vmem)
    return pl.pallas_call(
        functools.partial(finish_kernel, factor),
        out_shape=[
            jax.ShapeDtypeStruct((2048, 512), HALF),
            jax.ShapeDtypeStruct((256, 512), HALF),
        ]
        + [jax.ShapeDtypeStruct((512, 512), FULL)] * 6
        + [jax.ShapeDtypeStruct((512,), FULL)],
        in_specs=[anywhere] * 3 + [near],
        out_specs=[anywhere] * 8 + [near],
        scratch_shapes=[
            vmem((6, 512, 512), HALF),
            vmem((6, 512, 512), FULL),
            vmem((2048, 512), HALF),
            vmem((256, 512), HALF),
            pltpu.SemaphoreType.DMA((6,)),
            pltpu.SemaphoreType.DMA((6,)),
            pltpu.SemaphoreType.DMA((4,)),
        ],
        compiler_params=pltpu.CompilerParams(vmem_limit_bytes=62 * 1024 * 1024),
    )(grid_grad, mesh_grad, totals, gain_total)


def shards(
    grid_latent,
    mesh_init,
    cotangent,
    enc_senders,
    enc_counts,
    dec_senders,
    recv_weight,
    send_weight,
    update_weight,
    norm_gain,
    mesh_send_weight,
    grid_recv_weight,
    output_weight,
):
    grid_grad, mesh_grad, totals, gain_total = everything(
        grid_latent[0],
        mesh_init[0],
        cotangent[0],
        enc_senders,
        enc_counts,
        dec_senders,
        recv_weight,
        send_weight,
        update_weight,
        norm_gain,
        mesh_send_weight,
        grid_recv_weight,
        output_weight,
    )
    factor = 1.0 / math.sqrt(2048 * lax.axis_size("graph") * lax.axis_size("dp"))
    outs = finish(factor, grid_grad, mesh_grad, totals, gain_total)
    order = (6, 7, 4, 8, 5, 2, 3)
    return (outs[0][None], outs[1][None]) + tuple(outs[number] for number in order)


def solution(mesh):
    return jax.shard_map(
        shards,
        mesh=mesh,
        in_specs=(
            P("dp", "graph", None),
            P("dp", "graph", None),
            P("dp", "graph", None),
            P(None, "graph"),
            P("graph"),
            P(None, "graph"),
            P(),
            P(),
            P(),
            P(),
            P(),
            P(),
            P(),
        ),
        out_specs=(
            P("dp", "graph", None),
            P("dp", "graph", None),
            P(),
            P(),
            P(),
            P(),
            P(),
            P(),
            P(),
        ),
        check_vma=False,
    )
```
